128 devices in a mesh: expert: 64 (over y, x, z), head: 2 (over core).
Axes of the slice: x: 4, y: 4, z: 4, core: 2. Of those that a mesh axis runs over, the one named last changes fastest.
Arguments:
- tokens: bfloat16 [8192, 4096], P('expert'), may hold values from -6 to 6
- router_weight: bfloat16 [4096, 64], replicated, may hold values from -16 to 16
- gate_weight: bfloat16 [64, 4096, 1536], P('expert', None, 'head'), may hold values from -0.09375 to 0.09375
- up_weight: bfloat16 [64, 4096, 1536], P('expert', None, 'head'), may hold values from -0.09375 to 0.09375
- down_weight: bfloat16 [64, 1536, 4096], P('expert', 'head'), may hold values from -0.15625 to 0.15625
- head_weight: bfloat16 [4096], replicated, may hold values from -0.09375 to 0.09375
- expert_ids: int32 [8192, 8], P('expert'), may hold values from 0 to 63, all different within a row; in each aligned block of 128 rows (0 to 127, 128 to 255, ...) at most 18 rows name the same one
- lengths: int32 [64, 4], replicated, may hold values from 1 to 48, 128 in all within a row
- pairs: int32 [128, 2], replicated, may hold values from 0 to 255, as said below
Outputs:
- token_grad: bfloat16 [8192, 4096], P('expert', 'head')
The draws below stay inside these ranges and needn't reach their ends.
Inputs may be any that keep to these rules, and one draw needn't show every extreme that they name: `expert_ids`: each row names 8 different experts; among the rows of one group no expert is named more than 18 times. `lengths`: each row sums to 128. `pairs`: every sequence number appears exactly once.
All inputs are finite; a program needn't handle non-finite values.
Results may differ from the reference program's by a relative error of at most 0.02.
Values may be sent and summed in bfloat16 or wider, within the bound.
No kernel may reach another device: no remote copies, remote signals or barrier semaphores. Data moves between devices by JAX's collectives and lax.ppermute only.
A program may use at most 128 MiB of HBM per device.

```python
import math
import jax
import jax.numpy as jnp
import numpy as np
from jax import lax

D = 4096
FF = 1536
TOPK = 8
TOK_DEV = 128
SEQ_DEV = 4
LOSS_SCALE = 1024
EXPERTS = 64
GROUPS = 64
TOKENS = 8192
SEQS = 256
PAIRS = 128
CAP = 18
MAXLEN = 48
FFH = 768
N_HEAD = 2


def draw_router_weight(key, part):
    key = jax.random.fold_in(key, 11)
    normal_key = jax.random.fold_in(key, 0)
    values = jax.random.normal(normal_key, (D, EXPERTS), jnp.float32) * D ** (-0.5)
    return values.astype(jnp.bfloat16)


def draw_pairs(key, part):
    key = jax.random.fold_in(key, 23)
    order = jax.random.permutation(key, SEQS).astype(jnp.int32)
    return order.reshape(PAIRS, 2)


def shard_levels(own_key, dims, shards, low, high):
    factor_of, own = 1.0, jax.random.fold_in(own_key, 6)
    for dim, blocks in shards:
        draws = jnp.exp(jax.random.uniform(jax.random.fold_in(own, dim), (blocks,), jnp.float32, low / len(shards), high / len(shards)))
        factor_of = factor_of * jnp.repeat(draws, dims[dim] // blocks).reshape([-1 if axis == dim else 1 for axis in range(len(dims))])
    return factor_of


def profile(number_of, total, limit, slope):
    portions = [(1 << 20) // math.isqrt(grade ** slope) + 1 for grade in range(2, number_of + 1)]
    surplus, counts = total - limit - (number_of - 1), [1] * (number_of - 1)
    while surplus > 0:
        movable = [i for i in range(number_of - 1) if counts[i] < limit]
        whole, budget = sum([portions[i] for i in movable]), surplus
        for i in movable:
            addition = min(limit - counts[i], max(1, budget * portions[i] // whole), surplus)
            counts[i] = counts[i] + addition
            surplus = surplus - addition
    return np.array([limit] + counts)


def ragged(rng, number_of, total, limit, slope):
    if number_of == 2:
        one = jax.random.randint(rng, (), max(1, total - limit), min(limit, total - 1) + 1)
        return jnp.stack([one, total - one])
    sizes = jnp.asarray(profile(number_of, total, limit, slope), jnp.int32)
    pairs = (number_of - 1) // 2
    source_of, sink = sizes[1:1 + 2 * pairs:2], sizes[2:2 + 2 * pairs:2]
    room = jnp.minimum(source_of - 1, limit - sink)
    passed = jax.random.randint(jax.random.fold_in(rng, 1), (pairs,), 0, 1 << 20) % (room + 1)
    sizes = sizes.at[1:1 + 2 * pairs:2].set(source_of - passed).at[2:2 + 2 * pairs:2].set(sink + passed)
    return sizes[jax.random.permutation(jax.random.fold_in(rng, 2), number_of)]


def shared_out(rng, own, number, rows, count, top, reach, slope):
    ranking = jax.random.permutation(rng, count)
    heavy_load, usual = shares(count, rows * top, reach, slope, True), shares(count, rows * top, reach, slope, False)
    places = jnp.arange(count)

    def named(sizes, turn):
        used = int((sizes > 0).sum())
        fixed = max(1, used // 4)
        passed = fixed + (places - fixed + turn * (used - fixed)) % max(1, count - fixed)
        return jnp.zeros((count,), jnp.int32).at[ranking[jnp.where(places < fixed, places, passed)]].set(jnp.asarray(sizes, jnp.int32))

    sizes = jnp.where(number % 4 == 0, named(heavy_load, number // 4), named(usual, number - number // 4 - 1))
    mixed = jax.random.permutation(jax.random.fold_in(own, 3), count)
    source_of, taker = mixed[0:count // 2 * 2:2], mixed[1:count // 2 * 2:2]
    room = jnp.minimum(sizes[source_of] - 1, reach - sizes[taker]) // 2
    room = jnp.where((source_of == ranking[0]) | (taker == ranking[0]) | (sizes[taker] == 0), 0, jnp.maximum(room, 0))
    passed = jax.random.randint(jax.random.fold_in(own, 4), (count // 2,), 0, 1 << 20) % (room + 1)
    sizes = sizes.at[source_of].add(-passed).at[taker].add(passed)
    labels = jnp.searchsorted(jnp.cumsum(sizes), jnp.arange(rows * top), side="right").astype(jnp.int32)
    grid = labels.reshape(top, rows).T
    grid = grid[jax.random.permutation(jax.random.fold_in(own, 1), rows)]
    turn = jax.random.randint(jax.random.fold_in(own, 2), (rows, 1), 0, top)
    return jnp.take_along_axis(grid, (jnp.arange(top)[None, :] + turn) % top, axis=1)


def shares(count, total, limit, skew, full):
    weights = [(1 << 20) // math.isqrt(standing ** skew) + 1 for standing in range(1, count + 1)]
    largest = limit if full else min(limit, max(-(-total // count), total * weights[0] // sum(weights)))
    least = 1 if total - largest >= count - 1 else 0
    holding, spare = [largest] + [least] * (count - 1), total - largest - least * (count - 1)
    while spare > 0:
        movable = [i for i in range(1, count) if holding[i] < largest] or [i for i in range(1, count) if holding[i] < limit]
        mass, remaining = sum([weights[i] for i in movable]), spare
        for i in movable:
            extra = min(limit - holding[i], max(1, remaining * weights[i] // mass), spare)
            holding[i] = holding[i] + extra
            spare = spare - extra
    return np.array(holding)


def gaussian(own_key, shape, spread, bound, shards=(), held_as=jnp.bfloat16):
    level = shard_levels(own_key, shape, shards, -0.22, 0.18) if shards else 1.0
    array = jax.random.normal(own_key, shape, jnp.float32) * spread * level
    return jnp.minimum(jnp.maximum(array, -bound), bound).astype(held_as)


def setup_inputs(seed: int = 0) -> dict:
    keys = jax.random.split(jax.random.key(seed), 10)
    tokens = gaussian(keys[0], (TOKENS, D), 1.0, 6.0, ((0, 64),))
    router_weight = draw_router_weight(jax.random.fold_in(keys[9], 71), 0)
    gate_weight = gaussian(keys[2], (EXPERTS, D, FF), D ** -0.5, 0.09375, ((0, 64), (2, 2)))
    up_weight = gaussian(keys[3], (EXPERTS, D, FF), D ** -0.5, 0.09375, ((0, 64), (2, 2)))
    down_weight = gaussian(keys[4], (EXPERTS, FF, D), FF ** -0.5, 0.15625, ((0, 64), (1, 2)))
    head_weight = gaussian(keys[5], (D,), D ** -0.5, 0.09375)
    expert_ids_keys = jax.random.split(jax.random.fold_in(keys[6], 1), TOKENS // TOK_DEV)
    expert_ids_turns = jax.random.permutation(jax.random.fold_in(keys[6], 3), TOKENS // TOK_DEV)
    expert_ids = jax.vmap(lambda own, number: shared_out(jax.random.fold_in(keys[6], 2), own, number, TOK_DEV, EXPERTS, TOPK, CAP, 0))(expert_ids_keys, expert_ids_turns).reshape((TOKENS, TOPK))
    lengths = jax.vmap(lambda own: ragged(own, SEQ_DEV, TOK_DEV, MAXLEN, 1))(jax.random.split(keys[7], GROUPS)).reshape((GROUPS, SEQ_DEV)).astype(jnp.int32)
    pairs = draw_pairs(jax.random.fold_in(keys[9], 71), 0)
    return {"tokens": tokens, "router_weight": router_weight, "gate_weight": gate_weight, "up_weight": up_weight, "down_weight": down_weight, "head_weight": head_weight, "expert_ids": expert_ids, "lengths": lengths, "pairs": pairs}


def route_slots(group_ids, experts, capacity):
    flat_ids = group_ids.reshape(-1)
    onehot = (flat_ids[:, None] == jnp.arange(experts, dtype=jnp.int32)[None, :]).astype(jnp.int32)
    before = jnp.cumsum(onehot, axis=0) - onehot
    slot_index = jnp.sum(before * onehot, axis=1)
    return flat_ids * capacity + slot_index


def segment_table(row_lengths, token_count):
    seq_ends = jnp.cumsum(row_lengths)
    seq_starts = seq_ends - row_lengths
    positions = jnp.arange(token_count, dtype=jnp.int32)[:, None]
    return ((positions >= seq_starts[None, :]) & (positions < seq_ends[None, :])).astype(jnp.float32)


def fit_moments(values, seq_lengths, moment_zero, moment_one, seq_count, len_sum, len_square):
    determinant = seq_count * len_square - len_sum * len_sum
    slope_fit = (seq_count * moment_one - len_sum * moment_zero) / determinant
    offset_fit = (moment_zero - slope_fit * len_sum) / seq_count
    return values - offset_fit - slope_fit * seq_lengths


def fit_all(values, seq_lengths):
    seq_count = jnp.float32(values.shape[0])
    return fit_moments(values, seq_lengths, jnp.sum(values), jnp.sum(values * seq_lengths), seq_count,
                       jnp.sum(seq_lengths), jnp.sum(seq_lengths * seq_lengths))


def reference(tokens, router_weight, gate_weight, up_weight, down_weight, head_weight, expert_ids, lengths, pairs):
    grouped_ids = expert_ids.reshape(GROUPS, TOK_DEV, TOPK)
    local_pos = jax.vmap(lambda group_ids: route_slots(group_ids, EXPERTS, CAP))(grouped_ids)
    group_col = jnp.arange(GROUPS, dtype=jnp.int32)[:, None]
    global_pos = (local_pos // CAP) * (GROUPS * CAP) + group_col * CAP + local_pos % CAP
    owner_token = group_col * TOK_DEV + jnp.arange(TOK_DEV * TOPK, dtype=jnp.int32)[None, :] // TOPK
    flat_pos = global_pos.reshape(-1)
    slot_owner = jnp.zeros((EXPERTS * GROUPS * CAP,), jnp.int32).at[flat_pos].set(owner_token.reshape(-1) + 1)
    slot_owner = slot_owner.reshape(EXPERTS, GROUPS * CAP)

    def forward_expert(inputs):
        owners, w_gate, w_up, w_down = inputs
        is_filled = owners > 0
        row_block = jnp.where(is_filled[:, None], tokens[jnp.maximum(owners - 1, 0)], 0.0).astype(tokens.dtype)
        gate_pre = jnp.dot(row_block, w_gate, preferred_element_type=jnp.float32)
        up_pre = jnp.dot(row_block, w_up, preferred_element_type=jnp.float32)
        hidden = (jax.nn.silu(gate_pre) * up_pre).astype(jnp.bfloat16)
        hidden = lax.optimization_barrier(hidden)
        head_map = jnp.dot(w_down, head_weight, preferred_element_type=jnp.float32)
        scores = jnp.sum(hidden.astype(jnp.float32) * head_map[None, :], axis=1)
        return gate_pre, up_pre, scores

    gate_all, up_all, score_all = lax.map(forward_expert, (slot_owner, gate_weight, up_weight, down_weight))
    scores = score_all.reshape(-1)[flat_pos].reshape(TOKENS, TOPK)

    logits = jnp.dot(tokens, router_weight, preferred_element_type=jnp.float32)
    picked = jnp.take_along_axis(logits, expert_ids, axis=1)
    route_prob = jax.nn.softmax(picked, axis=1)
    base_term = jnp.dot(tokens, head_weight, preferred_element_type=jnp.float32)
    value = base_term + jnp.sum(route_prob * scores, axis=1)

    member = jax.vmap(lambda row_lengths: segment_table(row_lengths, TOK_DEV))(lengths)
    group_lengths = lengths.astype(jnp.float32)
    reward = jnp.einsum('gts,gt->gs', member, value.reshape(GROUPS, TOK_DEV),
                        precision=lax.Precision.HIGHEST) / group_lengths
    seq_lengths = group_lengths.reshape(-1)
    residual = fit_all(reward.reshape(-1), seq_lengths)

    margin = residual[pairs[:, 0]] - residual[pairs[:, 1]]
    pull = LOSS_SCALE * jax.nn.sigmoid(-margin)
    reward_grad = jnp.zeros((SEQS,), jnp.float32).at[pairs[:, 0]].add(-pull).at[pairs[:, 1]].add(pull)
    grad_back = fit_all(reward_grad, seq_lengths)
    token_coef = jnp.einsum('gts,gs->gt', member, grad_back.reshape(GROUPS, SEQ_DEV) / group_lengths,
                            precision=lax.Precision.HIGHEST).reshape(TOKENS)

    dprob = token_coef[:, None] * scores
    dpicked = route_prob * (dprob - jnp.sum(route_prob * dprob, axis=1, keepdims=True))
    expert_hits = (expert_ids[:, :, None] == jnp.arange(EXPERTS, dtype=jnp.int32)[None, None, :]).astype(jnp.float32)
    dlogits = jnp.sum(dpicked[:, :, None] * expert_hits, axis=1).astype(jnp.bfloat16)
    router_term = lax.dot_general(dlogits, router_weight, (((1,), (1,)), ((), ())), preferred_element_type=jnp.float32)

    dscore = (token_coef[:, None] * route_prob).reshape(-1)
    dscore_all = jnp.zeros((EXPERTS * GROUPS * CAP,), jnp.float32).at[flat_pos].set(dscore)
    dscore_all = dscore_all.reshape(EXPERTS, GROUPS * CAP)

    def backward_expert(accumulated, inputs):
        owners, gate_pre, up_pre, dscore_rows, w_gate, w_up, w_down = inputs
        head_map = jnp.dot(w_down, head_weight, preferred_element_type=jnp.float32)
        gate_sigmoid = jax.nn.sigmoid(gate_pre)
        act_value = gate_pre * gate_sigmoid
        act_slope = gate_sigmoid * (1.0 + gate_pre * (1.0 - gate_sigmoid))
        dhidden = dscore_rows[:, None] * head_map[None, :]
        d_up = (dhidden * act_value).astype(jnp.bfloat16)
        d_gate = (dhidden * up_pre * act_slope).astype(jnp.bfloat16)
        summed_dx = jnp.zeros((owners.shape[0], D), jnp.float32)
        for half_index in range(N_HEAD):
            lower = half_index * FFH
            partial_dx = lax.dot_general(d_gate[:, lower:lower + FFH], w_gate[:, lower:lower + FFH],
                                         (((1,), (1,)), ((), ())), preferred_element_type=jnp.float32)
            partial_dx = partial_dx + lax.dot_general(d_up[:, lower:lower + FFH], w_up[:, lower:lower + FFH],
                                                      (((1,), (1,)), ((), ())), preferred_element_type=jnp.float32)
            rounded = lax.optimization_barrier(partial_dx.astype(jnp.bfloat16))
            summed_dx = summed_dx + rounded.astype(jnp.float32)
        is_filled = owners > 0
        accumulated = accumulated.at[jnp.maximum(owners - 1, 0)].add(jnp.where(is_filled[:, None], summed_dx, 0.0))
        return accumulated, None

    expert_term, _ = lax.scan(backward_expert, jnp.zeros((TOKENS, D), jnp.float32),
                              (slot_owner, gate_all, up_all, dscore_all, gate_weight, up_weight, down_weight))
    total = expert_term + token_coef[:, None] * head_weight.astype(jnp.float32)[None, :] + router_term
    return total.astype(jnp.bfloat16)
```

```python
import jax
import jax.numpy as jnp
from jax import lax
from jax.sharding import PartitionSpec as P

LOSS_SCALE = 1024
MAIN = 8
LANES = 128
SWAP = [(0, 1), (1, 0)]
F32 = jnp.float32
BF16 = jnp.bfloat16


def split_three(x):
    high = lax.reduce_precision(x, 8, 7)
    middle = lax.reduce_precision(x - high, 8, 7)
    low = x - high - middle
    return high.astype(BF16), middle.astype(BF16), low.astype(BF16)


def fit_all(values, seq_lengths):
    n = jnp.float32(values.shape[0])
    s1 = jnp.sum(seq_lengths)
    s2 = jnp.sum(seq_lengths * seq_lengths)
    v0 = jnp.sum(values)
    v1 = jnp.sum(values * seq_lengths)
    slope = (n * v1 - s1 * v0) / (n * s2 - s1 * s1)
    offset = (v0 - slope * s1) / n
    return values - offset - slope * seq_lengths


def exchange(x):
    return lax.all_to_all(x, "expert", split_axis=0, concat_axis=0, tiled=True)


def swap(x):
    return lax.ppermute(x, "head", SWAP)


def expand(extra_mask, pieces):
    experts, toks = extra_mask.shape
    eye = jnp.eye(pieces, dtype=extra_mask.dtype)
    full = extra_mask[:, None, None, :] * eye[None, :, :, None]
    return full.reshape(experts * pieces, pieces * toks)


def per_device(
    tokens,
    router_weight,
    gate_weight,
    up_weight,
    down_weight,
    head_weight,
    expert_ids,
    lengths,
    pairs,
):
    toks, width = tokens.shape
    experts = router_weight.shape[1]
    groups = lengths.shape[0]
    seq_dev = lengths.shape[1]
    seqs = groups * seq_dev
    half = width // 2
    piece = half // MAIN
    cap = 2 * (MAIN + 1)
    me = lax.axis_index("expert")
    head = lax.axis_index("head")
    w_gate, w_up, w_down = gate_weight[0], up_weight[0], down_weight[0]

    expert_iota = jnp.arange(experts, dtype=jnp.int32)
    hit3 = expert_ids[:, :, None] == expert_iota[None, None, :]
    hits = jnp.any(hit3, axis=1).astype(BF16)
    tri = jnp.tril(jnp.ones((toks, toks), BF16), -1)
    before = jnp.dot(tri, hits, preferred_element_type=F32).astype(jnp.int32)
    slot_te = jnp.where(hits > 0, before, -1)
    slot_et = slot_te.T

    def masks(first, extra):
        slots = first + jnp.arange(MAIN, dtype=jnp.int32)
        main = (slot_et[:, None, :] == slots[None, :, None]).astype(BF16)
        return main.reshape(experts * MAIN, toks), (slot_et == extra).astype(BF16)

    mask_a = masks(0, 2 * MAIN)
    mask_b = masks(MAIN, 2 * MAIN + 1)
    tok_half = lax.dynamic_slice_in_dim(tokens, head * half, half, 1)
    tok_pieces = tok_half.reshape(toks, MAIN, piece).transpose(1, 0, 2).reshape(MAIN * toks, piece)

    def gather_rows(mask):
        main = jnp.dot(mask[0], tok_half, preferred_element_type=F32).astype(BF16)
        extra = jnp.dot(expand(mask[1], MAIN), tok_pieces, preferred_element_type=F32).astype(BF16)
        return jnp.concatenate(
            [main.reshape(experts, MAIN, half), extra.reshape(experts, MAIN, piece)], axis=2
        )

    recv_a = exchange(gather_rows(mask_a))

    logits = jnp.dot(tokens, router_weight, preferred_element_type=F32)
    masked = jnp.where(hits > 0, logits, -jnp.inf)
    top = jnp.max(masked, axis=1, keepdims=True)
    weights = jnp.where(hits > 0, jnp.exp(logits - top), 0.0)
    prob = weights / jnp.sum(weights, axis=1, keepdims=True)
    own_lengths = lax.dynamic_slice_in_dim(lengths, me, 1, 0)[0]
    ends = jnp.cumsum(own_lengths)
    starts = ends - own_lengths
    position = jnp.arange(toks, dtype=jnp.int32)[:, None]
    member = ((position >= starts[None, :]) & (position < ends[None, :])).astype(F32)
    own_float = own_lengths.astype(F32)
    seq_of = jnp.sum(member * jnp.arange(seq_dev, dtype=F32)[None, :], axis=1)
    inv_len = jnp.sum(member / own_float[None, :], axis=1)

    slot_iota = jnp.arange(cap, dtype=jnp.int32)
    at_slot = slot_et[:, None, :] == slot_iota[None, :, None]
    weight_et = (prob * inv_len[:, None]).T
    weight_slot = jnp.sum(jnp.where(at_slot, weight_et[:, None, :], 0.0), axis=2)
    seq_slot = jnp.sum(jnp.where(at_slot, seq_of[None, None, :], 0.0), axis=2)
    side = jnp.concatenate([*split_three(weight_slot), seq_slot.astype(BF16)], axis=1)
    side = jnp.pad(side, ((0, 0), (0, LANES - 4 * cap)))
    side = jnp.pad(side[:, None, :], ((0, 0), (0, MAIN - 1), (0, 0)))
    recv_b = exchange(jnp.concatenate([gather_rows(mask_b), side], axis=2))

    head_map = jnp.dot(w_down, head_weight, preferred_element_type=F32)
    base = jnp.dot(tokens, head_weight, preferred_element_type=F32)
    base_reward = jnp.sum(base[:, None] * member, axis=0) / own_float

    def order(own, other):
        low = jnp.where(head == 0, own, other)
        high = jnp.where(head == 0, other, own)
        return low, high

    def unpack(block):
        main = block[:, :, :half].reshape(groups * MAIN, half)
        extra = block[:, :, half : half + piece].reshape(groups, half)
        return jnp.concatenate([main, extra], axis=0)

    def pack(rows):
        main = rows[: groups * MAIN].reshape(groups, MAIN, half)
        extra = rows[groups * MAIN :].reshape(groups, MAIN, piece)
        return jnp.concatenate([main, extra], axis=2)

    def work(recv):
        own = recv[:, :, : half + piece]
        other = swap(own)
        low, high = order(unpack(own), unpack(other))
        rows = jnp.concatenate([low, high], axis=1)
        gate_pre = jnp.dot(rows, w_gate, preferred_element_type=F32)
        up_pre = jnp.dot(rows, w_up, preferred_element_type=F32)
        gate_sigmoid = jax.nn.sigmoid(gate_pre)
        act_value = gate_pre * gate_sigmoid
        hidden = (act_value * up_pre).astype(BF16)
        score = jnp.sum(hidden.astype(F32) * head_map[None, :], axis=1)
        act_slope = gate_sigmoid * (1.0 + gate_pre * (1.0 - gate_sigmoid))
        d_up = (head_map[None, :] * act_value).astype(BF16)
        d_gate = (head_map[None, :] * up_pre * act_slope).astype(BF16)

        def product(first_col):
            wg = lax.dynamic_slice_in_dim(w_gate, first_col, half, 0)
            wu = lax.dynamic_slice_in_dim(w_up, first_col, half, 0)
            dims = (((1,), (1,)), ((), ()))
            return lax.dot_general(
                d_gate, wg, dims, preferred_element_type=F32
            ) + lax.dot_general(d_up, wu, dims, preferred_element_type=F32)

        away = pack(product((1 - head) * half).astype(BF16))
        keep = pack(product(head * half).astype(BF16))
        back = swap(away)
        total = (keep.astype(F32) + back.astype(F32)).astype(BF16)
        score_main = score[: groups * MAIN].reshape(groups, MAIN)
        return total, score_main, score[groups * MAIN :].reshape(groups, 1)

    total_a, main_a, extra_a = work(recv_a)
    total_b, main_b, extra_b = work(recv_b)
    score_half = jnp.concatenate([main_a, main_b, extra_a, extra_b], axis=1)
    score_rows = score_half + swap(score_half)

    side_in = recv_b[:, 0, half + piece :].astype(F32)
    weight_in = side_in[:, :cap] + side_in[:, cap : 2 * cap] + side_in[:, 2 * cap : 3 * cap]
    seq_in = side_in[:, 3 * cap : 4 * cap]
    weighted = weight_in * score_rows
    parts = [
        jnp.sum(jnp.where(seq_in == float(j), weighted, 0.0), axis=1) for j in range(seq_dev)
    ]
    partial_reward = jnp.stack(parts, axis=1)
    own_row = (jnp.arange(groups, dtype=jnp.int32) == me)[:, None]
    partial_reward = partial_reward + jnp.where(own_row, base_reward[None, :], 0.0)
    reward_lines = jnp.concatenate(split_three(partial_reward.reshape(seqs // LANES, LANES)), axis=0)
    reward_lines = jnp.broadcast_to(reward_lines[None], (groups,) + reward_lines.shape)
    score_line = jnp.concatenate(split_three(score_rows), axis=1)
    score_line = jnp.pad(score_line, ((0, 0), (0, LANES - 3 * cap)))[:, None, :]
    filler = jnp.zeros((groups, MAIN - 1 - reward_lines.shape[1], LANES), BF16)
    side_back = jnp.concatenate([reward_lines, score_line, filler], axis=1)

    home_a = exchange(total_a)
    home_b = exchange(jnp.concatenate([total_b, side_back], axis=2))

    prob_et = prob.T
    prob_high = lax.reduce_precision(prob_et, 8, 7)
    prob_parts = (prob_high.astype(BF16), (prob_et - prob_high).astype(BF16))

    def combine(mask, home):
        main = home[:, :, :half].reshape(experts * MAIN, half)
        extra = home[:, :, half : half + piece].reshape(experts * MAIN, piece)
        out = 0.0
        for part in prob_parts:
            left = (mask[0].reshape(experts, MAIN, toks) * part[:, None, :]).reshape(-1, toks)
            out = out + lax.dot_general(
                left, main, (((0,), (0,)), ((), ())), preferred_element_type=F32
            )
            spread = lax.dot_general(
                expand(mask[1] * part, MAIN),
                extra,
                (((0,), (0,)), ((), ())),
                preferred_element_type=F32,
            )
            out = out + spread.reshape(MAIN, toks, piece).transpose(1, 0, 2).reshape(toks, half)
        return out

    expert_term = combine(mask_a, home_a) + combine(mask_b, home_b)

    side_home = home_b[:, :, half + piece :].astype(F32)
    lines = seqs // LANES
    totals = jnp.sum(side_home, axis=0)
    reward = (totals[:lines] + totals[lines : 2 * lines] + totals[2 * lines : 3 * lines]).reshape(seqs)
    score_parts = side_home[:, 3 * lines, :]
    score_es = score_parts[:, :cap] + score_parts[:, cap : 2 * cap] + score_parts[:, 2 * cap : 3 * cap]
    score_te = jnp.sum(jnp.where(at_slot, score_es[:, :, None], 0.0), axis=1).T
    seq_lengths = lengths.astype(F32).reshape(-1)
    residual = fit_all(reward, seq_lengths)
    seq_numbers = jnp.arange(seqs, dtype=jnp.int32)[None, :]
    chosen = (pairs[:, 0:1] == seq_numbers).astype(F32)
    rejected = (pairs[:, 1:2] == seq_numbers).astype(F32)
    margin = jnp.sum((chosen - rejected) * residual[None, :], axis=1)
    pull = LOSS_SCALE * jax.nn.sigmoid(-margin)
    reward_grad = jnp.sum(pull[:, None] * (rejected - chosen), axis=0)
    grad_back = fit_all(reward_grad, seq_lengths)
    own_grad = lax.dynamic_slice_in_dim(grad_back, me * seq_dev, seq_dev, 0)
    token_coef = jnp.sum(member * (own_grad / own_float)[None, :], axis=1)

    mean_score = jnp.sum(prob * score_te, axis=1, keepdims=True)
    dlogits = (prob * (score_te - mean_score)).astype(BF16)
    router_half = lax.dynamic_slice_in_dim(router_weight, head * half, half, 0)
    router_term = lax.dot_general(
        dlogits, router_half, (((1,), (1,)), ((), ())), preferred_element_type=F32
    )
    head_half = lax.dynamic_slice_in_dim(head_weight, head * half, half, 0).astype(F32)
    return (token_coef[:, None] * (expert_term + router_term + head_half[None, :])).astype(BF16)


def solution(mesh):
    return jax.shard_map(
        per_device,
        mesh=mesh,
        in_specs=(
            P("expert", None),
            P(),
            P("expert", None, "head"),
            P("expert", None, "head"),
            P("expert", "head", None),
            P(),
            P("expert", None),
            P(),
            P(),
        ),
        out_specs=P("expert", "head"),
        check_vma=False,
    )
```

```python
import functools

import jax
import jax.numpy as jnp
from jax import lax
from jax.experimental import pallas as pl
from jax.experimental.pallas import tpu as pltpu
from jax.sharding import PartitionSpec as P

LOSS_SCALE = 1024
MAIN = 8
LANES = 128
SWAP = [(0, 1), (1, 0)]
F32 = jnp.float32
BF16 = jnp.bfloat16


def split_three(x):
    high = lax.reduce_precision(x, 8, 7)
    middle = lax.reduce_precision(x - high, 8, 7)
    low = x - high - middle
    return high.astype(BF16), middle.astype(BF16), low.astype(BF16)


def exchange(x):
    return lax.all_to_all(x, "expert", split_axis=0, concat_axis=0, tiled=True)


def swap(x):
    return lax.ppermute(x, "head", SWAP)


def pick(rows, cols, first, axis):
    a = lax.broadcasted_iota(jnp.int32, (rows, cols), axis)
    b = lax.broadcasted_iota(jnp.int32, (rows, cols), 1 - axis)
    return (b == a * MAIN + first).astype(BF16)


def touch_kernel(*refs):
    pass


def touch(x, *after):
    return pl.pallas_call(
        touch_kernel,
        out_shape=jax.ShapeDtypeStruct(x.shape, x.dtype),
        in_specs=[pl.BlockSpec(memory_space=pl.ANY)] * (1 + len(after)),
        out_specs=pl.BlockSpec(memory_space=pl.ANY),
        input_output_aliases={0: 0},
    )(x, *after)


def expert_kernel(
    span,
    steps,
    head_ref,
    own_ref,
    other_ref,
    wg_ref,
    wu_ref,
    hm_ref,
    after_ref,
    keep_ref,
    away_ref,
    score_ref,
    x_ref,
    gate_ref,
    up_ref,
    dg_ref,
    du_ref,
):
    step = pl.program_id(0)
    main_rows = own_ref.shape[0]
    groups = main_rows // MAIN
    half = steps // 2 * span
    piece = half // MAIN
    pieces = span // piece

    def fill(src, chunk):
        x_ref[:main_rows, :] = src[:, pl.ds(pl.multiple_of(chunk * span, span), span)]
        extra = src[:, half : half + piece]
        for j in range(pieces):
            chosen = pick(groups, main_rows, chunk * pieces + j, 0)
            x_ref[main_rows:, j * piece : (j + 1) * piece] = jnp.dot(
                chosen, extra, preferred_element_type=F32
            ).astype(BF16)

    @pl.when(step < steps // 2)
    def _():
        fill(own_ref, step)

    @pl.when((step >= steps // 2) & (step < steps))
    def _():
        fill(other_ref, step - steps // 2)

    @pl.when(step == 0)
    def _():
        gate_ref[...] = jnp.dot(x_ref[...], wg_ref[...], preferred_element_type=F32)
        up_ref[...] = jnp.dot(x_ref[...], wu_ref[...], preferred_element_type=F32)

    @pl.when((step > 0) & (step < steps))
    def _():
        gate_ref[...] += jnp.dot(x_ref[...], wg_ref[...], preferred_element_type=F32)
        up_ref[...] += jnp.dot(x_ref[...], wu_ref[...], preferred_element_type=F32)

    @pl.when(step == steps - 1)
    def _():
        block = 64
        head_map = hm_ref[...]

        def body(i, carry):
            rows = pl.ds(pl.multiple_of(i * block, block), block)
            gate = gate_ref[rows, :]
            up = up_ref[rows, :]
            sig = 1.0 / (1.0 + jnp.exp(-gate))
            act = gate * sig
            hidden = (act * up).astype(BF16).astype(F32)
            score_ref[rows, :] = jnp.sum(hidden * head_map, axis=1, keepdims=True)
            du_ref[rows, :] = (head_map * act).astype(BF16)
            dg_ref[rows, :] = (head_map * up * sig * (1.0 + gate * (1.0 - sig))).astype(BF16)
            return carry

        lax.fori_loop(0, gate_ref.shape[0] // block, body, 0)

    def product():
        dims = (((1,), (1,)), ((), ()))
        return (
            lax.dot_general(dg_ref[...], wg_ref[...], dims, preferred_element_type=F32)
            + lax.dot_general(du_ref[...], wu_ref[...], dims, preferred_element_type=F32)
        ).astype(BF16)

    def store(dst, chunk):
        value = product()
        dst[:, pl.ds(pl.multiple_of(chunk * span, span), span)] = value[:main_rows]
        spread = 0.0
        for j in range(pieces):
            chosen = pick(main_rows, groups, chunk * pieces + j, 1)
            spread = spread + jnp.dot(
                chosen, value[main_rows:, j * piece : (j + 1) * piece], preferred_element_type=F32
            )

        @pl.when(chunk == 0)
        def _():
            dst[:, half:] = spread.astype(BF16)

        @pl.when(chunk > 0)
        def _():
            dst[:, half:] = (dst[:, half:].astype(F32) + spread).astype(BF16)

    @pl.when((step >= steps) & (step < steps + steps // 2))
    def _():
        store(keep_ref, step - steps)

    @pl.when(step >= steps + steps // 2)
    def _():
        store(away_ref, step - steps - steps // 2)


def expert_call(head, own, other, w_gate, w_up, head_map, after):
    main_rows = own.shape[0]
    width, hidden = w_gate.shape
    half = width // 2
    lanes = half + half // MAIN
    span = 1024
    steps = width // span
    rows = main_rows + main_rows // MAIN

    def weight_at(i, head_ref):
        return (lax.rem(head_ref[0] * (steps // 2) + lax.rem(i, steps), steps), 0)

    fixed = lambda i, head_ref: (0, 0)
    return pl.pallas_call(
        functools.partial(expert_kernel, span, steps),
        grid_spec=pltpu.PrefetchScalarGridSpec(
            num_scalar_prefetch=1,
            grid=(2 * steps,),
            in_specs=[
                pl.BlockSpec((main_rows, lanes), fixed),
                pl.BlockSpec((main_rows, lanes), fixed),
                pl.BlockSpec((span, hidden), weight_at),
                pl.BlockSpec((span, hidden), weight_at),
                pl.BlockSpec((1, hidden), fixed),
                pl.BlockSpec(memory_space=pl.ANY),
            ],
            out_specs=[
                pl.BlockSpec((main_rows, lanes), fixed),
                pl.BlockSpec((main_rows, lanes), fixed),
                pl.BlockSpec((rows, 1), fixed),
            ],
            scratch_shapes=[
                pltpu.VMEM((rows, span), BF16),
                pltpu.VMEM((rows, hidden), F32),
                pltpu.VMEM((rows, hidden), F32),
                pltpu.VMEM((rows, hidden), BF16),
                pltpu.VMEM((rows, hidden), BF16),
            ],
        ),
        out_shape=[
            jax.ShapeDtypeStruct((main_rows, lanes), BF16),
            jax.ShapeDtypeStruct((main_rows, lanes), BF16),
            jax.ShapeDtypeStruct((rows, 1), F32),
        ],
        compiler_params=pltpu.CompilerParams(
            dimension_semantics=("arbitrary",), vmem_limit_bytes=44 << 20
        ),
        cost_estimate=pl.CostEstimate(
            flops=8 * rows * width * hidden,
            bytes_accessed=8 * width * hidden + 8 * main_rows * lanes,
            transcendentals=rows * hidden,
        ),
    )(head, own, other, w_gate, w_up, head_map, after)


def combiner(home_ref, slot_te, prob_te, first, extra_slot):
    rows = home_ref.shape[0]
    toks, experts = slot_te.shape
    half = home_ref.shape[1] // (LANES * (MAIN + 1)) * LANES * MAIN
    piece = half // MAIN
    a = lax.broadcasted_iota(jnp.int32, (experts, rows), 0)
    b = lax.broadcasted_iota(jnp.int32, (experts, rows), 1)
    spread = ((b >= a * MAIN) & (b < a * MAIN + MAIN)).astype(BF16)
    column = lax.broadcasted_iota(jnp.int32, (toks, rows), 1) % MAIN

    def repeat(x):
        return jnp.dot(x.astype(BF16), spread, preferred_element_type=F32)

    slot = repeat(slot_te)
    high = prob_te.astype(BF16)
    parts = (repeat(high), repeat(prob_te - high.astype(F32)))
    in_main = slot == (column + first).astype(F32)
    in_extra = slot == float(extra_slot)
    main = [jnp.where(in_main, p, 0.0).astype(BF16) for p in parts]

    def block(index):
        lo = index * 2 * piece
        rows_main = home_ref[:, lo : lo + 2 * piece]
        out = sum(jnp.dot(m, rows_main, preferred_element_type=F32) for m in main)
        extra = home_ref[:, half : half + piece]
        sides = []
        for q in (2 * index, 2 * index + 1):
            here = in_extra & (column == q)
            sides.append(
                sum(
                    jnp.dot(
                        jnp.where(here, p, 0.0).astype(BF16), extra, preferred_element_type=F32
                    )
                    for p in parts
                )
            )
        return out + jnp.concatenate(sides, axis=1)

    return block, 2 * piece


def first_combine_kernel(home_ref, slot_ref, prob_ref, line_ref, out_ref):
    block, width = combiner(home_ref, slot_ref[...], prob_ref[...], 0, 2 * MAIN)
    for i in range(out_ref.shape[1] // width):
        cols = slice(i * width, (i + 1) * width)
        out_ref[:, cols] = block(i) + line_ref[:, cols]


def fit_line(values, seq_lengths):
    n = float(values.shape[1])
    s1 = jnp.sum(seq_lengths, axis=1, keepdims=True)
    s2 = jnp.sum(seq_lengths * seq_lengths, axis=1, keepdims=True)
    v0 = jnp.sum(values, axis=1, keepdims=True)
    v1 = jnp.sum(values * seq_lengths, axis=1, keepdims=True)
    slope = (n * v1 - s1 * v0) / (n * s2 - s1 * s1)
    offset = (v0 - slope * s1) / n
    return values - offset - slope * seq_lengths


def last_combine_kernel(
    cap,
    home_ref,
    slot_ref,
    prob_ref,
    slot_et_ref,
    prob_et_ref,
    acc_ref,
    router_ref,
    lens_ref,
    pairs_ref,
    member_ref,
    out_ref,
):
    rows = home_ref.shape[0]
    experts = rows // MAIN
    seqs = lens_ref.shape[1]
    lines = seqs // LANES
    side = home_ref[:, home_ref.shape[1] - LANES :]
    chosen = pick(experts, rows, 3 * lines, 0)
    packed = jnp.dot(chosen, side, preferred_element_type=F32)
    score_es = (
        packed
        + pltpu.roll(packed, LANES - cap, 1)
        + pltpu.roll(packed, LANES - 2 * cap, 1)
    )
    slot_et = slot_et_ref[...]
    prob_et = prob_et_ref[...]
    score_et = jnp.zeros_like(prob_et)
    for c in range(cap):
        score_et = score_et + jnp.where(slot_et == float(c), score_es[:, c : c + 1], 0.0)
    mean_score = jnp.sum(prob_et * score_et, axis=0, keepdims=True)
    dlogits = (prob_et * (score_et - mean_score)).astype(BF16)
    totals = jnp.sum(side.astype(F32).reshape(experts, MAIN, LANES), axis=0)
    totals = totals[:lines] + totals[lines : 2 * lines] + totals[2 * lines : 3 * lines]
    reward = jnp.concatenate([totals[i : i + 1] for i in range(lines)], axis=1)
    lens = lens_ref[...]
    residual = fit_line(reward, lens)
    numbers = lax.broadcasted_iota(jnp.int32, (pairs_ref.shape[0], seqs), 1)
    delta = (numbers == pairs_ref[:, 0:1]).astype(F32) - (numbers == pairs_ref[:, 1:2]).astype(F32)
    margin = jnp.sum(delta * residual, axis=1, keepdims=True)
    pull = LOSS_SCALE / (1.0 + jnp.exp(margin))
    reward_grad = -jnp.sum(pull * delta, axis=0, keepdims=True)
    grad_back = fit_line(reward_grad, lens)
    coef = jnp.sum(member_ref[...] * grad_back, axis=1, keepdims=True)

    block, width = combiner(home_ref, slot_ref[...], prob_ref[...], MAIN, 2 * MAIN + 1)
    for i in range(out_ref.shape[1] // width):
        cols = slice(i * width, (i + 1) * width)
        router_term = lax.dot_general(
            dlogits, router_ref[:, cols], (((0,), (0,)), ((), ())), preferred_element_type=F32
        )
        out_ref[:, cols] = (coef * (block(i) + acc_ref[:, cols] + router_term)).astype(BF16)


def expand(extra_mask, pieces):
    experts, toks = extra_mask.shape
    eye = jnp.eye(pieces, dtype=extra_mask.dtype)
    full = extra_mask[:, None, None, :] * eye[None, :, :, None]
    return full.reshape(experts * pieces, pieces * toks)


def per_device(
    tokens,
    router_weight,
    gate_weight,
    up_weight,
    down_weight,
    head_weight,
    expert_ids,
    lengths,
    pairs,
):
    toks, width = tokens.shape
    experts = router_weight.shape[1]
    groups = lengths.shape[0]
    seq_dev = lengths.shape[1]
    seqs = groups * seq_dev
    half = width // 2
    piece = half // MAIN
    cap = 2 * (MAIN + 1)
    me = lax.axis_index("expert")
    head = lax.axis_index("head")
    w_gate, w_up, w_down = gate_weight[0], up_weight[0], down_weight[0]

    expert_iota = jnp.arange(experts, dtype=jnp.int32)
    hit3 = expert_ids[:, :, None] == expert_iota[None, None, :]
    hits = jnp.any(hit3, axis=1).astype(BF16)
    tri = jnp.tril(jnp.ones((toks, toks), BF16), -1)
    before = jnp.dot(tri, hits, preferred_element_type=F32).astype(jnp.int32)
    slot_te = jnp.where(hits > 0, before, -1)
    slot_et = slot_te.T

    def masks(first, extra):
        slots = first + jnp.arange(MAIN, dtype=jnp.int32)
        main = (slot_et[:, None, :] == slots[None, :, None]).astype(BF16)
        return main.reshape(experts * MAIN, toks), (slot_et == extra).astype(BF16)

    mask_a = masks(0, 2 * MAIN)
    mask_b = masks(MAIN, 2 * MAIN + 1)
    tok_half = lax.dynamic_slice_in_dim(tokens, head * half, half, 1)
    tok_pieces = tok_half.reshape(toks, MAIN, piece).transpose(1, 0, 2).reshape(MAIN * toks, piece)

    def gather_rows(mask):
        main = jnp.dot(mask[0], tok_half, preferred_element_type=F32).astype(BF16)
        extra = jnp.dot(expand(mask[1], MAIN), tok_pieces, preferred_element_type=F32).astype(BF16)
        return jnp.concatenate(
            [main.reshape(experts, MAIN, half), extra.reshape(experts, MAIN, piece)], axis=2
        )

    recv_a = exchange(gather_rows(mask_a))

    logits = jnp.dot(tokens, router_weight, preferred_element_type=F32)
    masked = jnp.where(hits > 0, logits, -jnp.inf)
    top = jnp.max(masked, axis=1, keepdims=True)
    weights = jnp.where(hits > 0, jnp.exp(logits - top), 0.0)
    prob = weights / jnp.sum(weights, axis=1, keepdims=True)
    own_lengths = lax.dynamic_slice_in_dim(lengths, me, 1, 0)[0]
    ends = jnp.cumsum(own_lengths)
    starts = ends - own_lengths
    position = jnp.arange(toks, dtype=jnp.int32)[:, None]
    member = ((position >= starts[None, :]) & (position < ends[None, :])).astype(F32)
    own_float = own_lengths.astype(F32)
    seq_of = jnp.sum(member * jnp.arange(seq_dev, dtype=F32)[None, :], axis=1)
    inv_len = jnp.sum(member / own_float[None, :], axis=1)

    slot_iota = jnp.arange(cap, dtype=jnp.int32)
    at_slot = slot_et[:, None, :] == slot_iota[None, :, None]
    weight_et = (prob * inv_len[:, None]).T
    weight_slot = jnp.sum(jnp.where(at_slot, weight_et[:, None, :], 0.0), axis=2)
    seq_slot = jnp.sum(jnp.where(at_slot, seq_of[None, None, :], 0.0), axis=2)
    side = jnp.concatenate([*split_three(weight_slot), seq_slot.astype(BF16)], axis=1)
    side = jnp.pad(side, ((0, 0), (0, LANES - 4 * cap)))
    side = jnp.pad(side[:, None, :], ((0, 0), (0, MAIN - 1), (0, 0)))
    block_b = jnp.concatenate([gather_rows(mask_b), side], axis=2)
    recv_b = exchange(block_b)

    head_map = jnp.dot(w_down, head_weight, preferred_element_type=F32)
    base = jnp.dot(tokens, head_weight, preferred_element_type=F32)
    base_reward = jnp.sum(base[:, None] * member, axis=0) / own_float

    head_line = head_map[None, :]
    head_number = head.astype(jnp.int32)[None]
    main_rows = groups * MAIN

    def work(recv, other, after):
        own = recv.reshape(main_rows, -1)
        keep, away, score = expert_call(
            head_number, own, other.reshape(main_rows, -1), w_gate, w_up, head_line, after
        )
        score = score[:, 0]
        return keep, away, score[:main_rows].reshape(groups, MAIN), score[main_rows:, None]

    def finish(keep, away):
        back = swap(away)
        return (keep.astype(F32) + back.astype(F32)).astype(BF16).reshape(groups, MAIN, -1)

    recv_a = touch(recv_a, block_b, head_line)
    keep_a, away_a, main_a, extra_a = work(recv_a, swap(recv_a), head_line)
    recv_b = touch(recv_b, keep_a)
    total_a = finish(keep_a, away_a)
    keep_b, away_b, main_b, extra_b = work(recv_b, swap(recv_b), total_a)
    home_a = exchange(total_a)
    total_b = finish(keep_b, touch(away_b, home_a))
    score_half = jnp.concatenate([main_a, main_b, extra_a, extra_b], axis=1)
    score_rows = score_half + swap(score_half)

    side_in = recv_b[:, 0, half + piece :].astype(F32)
    weight_in = side_in[:, :cap] + side_in[:, cap : 2 * cap] + side_in[:, 2 * cap : 3 * cap]
    seq_in = side_in[:, 3 * cap : 4 * cap]
    weighted = weight_in * score_rows
    parts = [
        jnp.sum(jnp.where(seq_in == float(j), weighted, 0.0), axis=1) for j in range(seq_dev)
    ]
    partial_reward = jnp.stack(parts, axis=1)
    own_row = (jnp.arange(groups, dtype=jnp.int32) == me)[:, None]
    partial_reward = partial_reward + jnp.where(own_row, base_reward[None, :], 0.0)
    reward_lines = jnp.concatenate(split_three(partial_reward.reshape(seqs // LANES, LANES)), axis=0)
    reward_lines = jnp.broadcast_to(reward_lines[None], (groups,) + reward_lines.shape)
    score_line = jnp.concatenate(split_three(score_rows), axis=1)
    score_line = jnp.pad(score_line, ((0, 0), (0, LANES - 3 * cap)))[:, None, :]
    filler = jnp.zeros((groups, MAIN - 1 - reward_lines.shape[1], LANES), BF16)
    side_back = jnp.concatenate([reward_lines, score_line, filler], axis=1)

    home_b = exchange(jnp.concatenate([total_b, side_back], axis=2))

    vmem = pl.BlockSpec(memory_space=pltpu.VMEM)
    slot_f = slot_te.astype(F32)
    head_half = lax.dynamic_slice_in_dim(head_weight, head * half, half, 0).astype(F32)[None, :]
    acc = pl.pallas_call(
        first_combine_kernel,
        out_shape=jax.ShapeDtypeStruct((toks, half), F32),
        in_specs=[vmem] * 4,
        out_specs=vmem,
        compiler_params=pltpu.CompilerParams(vmem_limit_bytes=24 << 20),
    )(home_a.reshape(main_rows, -1), slot_f, prob, head_half)

    router_half = lax.dynamic_slice_in_dim(router_weight, head * half, half, 0).T
    own_seq = me * seq_dev + jnp.arange(seq_dev, dtype=jnp.int32)
    places = (jnp.arange(seqs, dtype=jnp.int32)[None, :] == own_seq[:, None]).astype(F32)
    member_line = jnp.sum((member / own_float[None, :])[:, :, None] * places[None], axis=1)
    return pl.pallas_call(
        functools.partial(last_combine_kernel, cap),
        out_shape=jax.ShapeDtypeStruct((toks, half), BF16),
        in_specs=[vmem] * 10,
        out_specs=vmem,
        compiler_params=pltpu.CompilerParams(vmem_limit_bytes=24 << 20),
    )(
        home_b.reshape(main_rows, -1),
        slot_f,
        prob,
        slot_et.astype(F32),
        prob.T,
        acc,
        router_half,
        lengths.astype(F32).reshape(1, seqs),
        pairs,
        member_line,
    )


def solution(mesh):
    return jax.shard_map(
        per_device,
        mesh=mesh,
        in_specs=(
            P("expert", None),
            P(),
            P("expert", None, "head"),
            P("expert", None, "head"),
            P("expert", "head", None),
            P(),
            P("expert", None),
            P(),
            P(),
        ),
        out_specs=P("expert", "head"),
        check_vma=False,
    )
```

```python
import functools

import jax
import jax.numpy as jnp
from jax import lax
from jax.experimental import pallas as pl
from jax.experimental.pallas import tpu as pltpu
from jax.sharding import PartitionSpec as P

LOSS_SCALE = 1024
MAIN = 8
LANES = 128
SWAP = [(0, 1), (1, 0)]
F32 = jnp.float32
BF16 = jnp.bfloat16


def split_three(x):
    high = lax.reduce_precision(x, 8, 7)
    middle = lax.reduce_precision(x - high, 8, 7)
    low = x - high - middle
    return high.astype(BF16), middle.astype(BF16), low.astype(BF16)


def exchange(x):
    return lax.all_to_all(x, "expert", split_axis=0, concat_axis=0, tiled=True)


def swap(x):
    return lax.ppermute(x, "head", SWAP)


def pick(rows, cols, first, axis):
    a = lax.broadcasted_iota(jnp.int32, (rows, cols), axis)
    b = lax.broadcasted_iota(jnp.int32, (rows, cols), 1 - axis)
    return (b == a * MAIN + first).astype(BF16)


def slot_order():
    return [*range(MAIN), 2 * MAIN, *range(MAIN, 2 * MAIN), 2 * MAIN + 1]


def pieces_of(x):
    high = x.astype(BF16)
    rest = x - high.astype(F32)
    middle = rest.astype(BF16)
    return high, middle, (rest - middle.astype(F32)).astype(BF16)


def spread_pieces(x, cap):
    line = jnp.zeros(x.shape, F32)
    for i, piece in enumerate(pieces_of(x)):
        piece = piece.astype(F32)
        line = line + (pltpu.roll(piece, i * cap, 1) if i else piece)
    return line.astype(BF16)


def join_pieces(line, cap):
    return (
        line + pltpu.roll(line, LANES - cap, 1) + pltpu.roll(line, LANES - 2 * cap, 1)
    )


def touch_kernel(*refs):
    pass


def touch(x, *after):
    return pl.pallas_call(
        touch_kernel,
        out_shape=jax.ShapeDtypeStruct(x.shape, x.dtype),
        in_specs=[pl.BlockSpec(memory_space=pl.ANY)] * (1 + len(after)),
        out_specs=pl.BlockSpec(memory_space=pl.ANY),
        input_output_aliases={0: 0},
    )(x, *after)


def expert_kernel(
    span,
    steps,
    cap,
    head_ref,
    own_hbm,
    other_hbm,
    wg_ref,
    wu_ref,
    hm_ref,
    before_ref,
    after_ref,
    keep_hbm,
    away_hbm,
    last_hbm,
    score_ref,
    own_ref,
    other_ref,
    keep_ref,
    away_ref,
    last_ref,
    x_ref,
    gate_ref,
    up_ref,
    dg_ref,
    du_ref,
    column_ref,
    stack_ref,
    in_sems,
    out_sems,
):
    step = pl.program_id(0)
    main_rows, lanes = own_ref.shape
    groups = main_rows // MAIN
    halves = steps // 2
    half = halves * span
    piece = half // MAIN
    pieces = span // piece

    def arrival(src, dst, cols, number):
        return pltpu.make_async_copy(src.at[:, cols], dst.at[:, cols], in_sems.at[number])

    blocks = [slice(i * span, (i + 1) * span) for i in range(halves)]
    tail = slice(half, lanes)
    own_cols = [*blocks, tail]

    def own_in(i):
        return arrival(own_hbm, own_ref, own_cols[i], i)

    def other_in():
        return arrival(other_hbm, other_ref, slice(0, lanes), halves + 1)

    def leaving(src, dst, number):
        return pltpu.make_async_copy(src, dst, out_sems.at[number])

    def keep_out(i):
        cols = own_cols[i]
        return leaving(keep_ref.at[:, cols], keep_hbm.at[:, cols], i)

    def away_out(i):
        cols = blocks[i]
        return leaving(away_ref.at[:, cols], away_hbm.at[:, cols], halves + 1 + i)

    def last_out():
        return leaving(last_ref, last_hbm, 2 * halves + 1)

    def shuffle():
        a = lax.broadcasted_iota(jnp.int32, (main_rows, main_rows), 0)
        b = lax.broadcasted_iota(jnp.int32, (main_rows, main_rows), 1)
        return (b == (a % groups) * MAIN + a // groups).astype(BF16)

    def gather_extra(src):
        stack_ref[...] = jnp.dot(
            shuffle(), src[:, half : half + piece], preferred_element_type=F32
        ).astype(BF16)

    def scatter_extra(dst, first):
        dims = (((0,), (0,)), ((), ()))
        dst[:, first : first + piece] = lax.dot_general(
            shuffle(), stack_ref[...], dims, preferred_element_type=F32
        ).astype(BF16)

    def fill(src, chunk):
        x_ref[:main_rows, :] = src[:, chunk * span : (chunk + 1) * span]
        for j in range(pieces):
            q = chunk * pieces + j
            x_ref[main_rows:, j * piece : (j + 1) * piece] = stack_ref[
                q * groups : (q + 1) * groups, :
            ]

    def forward(first):
        for acc, w in ((gate_ref, wg_ref), (up_ref, wu_ref)):
            value = jnp.dot(x_ref[...], w[...], preferred_element_type=F32)
            acc[...] = value if first else acc[...] + value

    for i in range(steps):

        @pl.when(step == i)
        def _(i=i):
            if i == 0:
                for number in (0, halves, *range(1, halves)):
                    own_in(number).start()
                other_in().start()
                own_in(halves).wait()
                gather_extra(own_ref)
            if i < halves:
                own_in(i).wait()
                fill(own_ref, i)
            else:
                if i == halves:
                    other_in().wait()
                    gather_extra(other_ref)
                fill(other_ref, i - halves)

    @pl.when(step == 0)
    def _():
        forward(True)

    @pl.when((step > 0) & (step < steps))
    def _():
        forward(False)

    @pl.when(step == steps - 1)
    def _():
        block = 64
        head_map = hm_ref[...]

        def body(i, carry):
            rows = pl.ds(pl.multiple_of(i * block, block), block)
            gate = gate_ref[rows, :]
            up = up_ref[rows, :]
            sig = 1.0 / (1.0 + jnp.exp(-gate))
            act = gate * sig
            hidden = (act * up).astype(BF16).astype(F32)
            column_ref[rows, :] = jnp.sum(hidden * head_map, axis=1, keepdims=True)
            du_ref[rows, :] = (head_map * act).astype(BF16)
            dg_ref[rows, :] = (head_map * up * sig * (1.0 + gate * (1.0 - sig))).astype(BF16)
            return carry

        lax.fori_loop(0, gate_ref.shape[0] // block, body, 0)
        place = lax.broadcasted_iota(jnp.int32, (main_rows, LANES), 0) % MAIN
        lane = lax.broadcasted_iota(jnp.int32, (main_rows, LANES), 1)
        table = jnp.where(lane == place, column_ref[:main_rows, :], 0.0)
        a = lax.broadcasted_iota(jnp.int32, (groups, main_rows), 0)
        b = lax.broadcasted_iota(jnp.int32, (groups, main_rows), 1)
        fold = ((b >= a * MAIN) & (b < a * MAIN + MAIN)).astype(BF16)
        folded = sum(jnp.dot(fold, t, preferred_element_type=F32) for t in pieces_of(table))
        lane = lax.broadcasted_iota(jnp.int32, (groups, LANES), 1)
        score = jnp.where(lane == MAIN, column_ref[main_rows:, :], folded)
        if cap is None:
            score_ref[...] = score
        else:
            score = jnp.where(lane <= MAIN, before_ref[...], pltpu.roll(score, MAIN + 1, 1))
            score = jnp.where(lane < cap, score, 0.0)
            score_ref[...] = score
            line = spread_pieces(score, cap)
            last_ref[:, span + piece :] = jnp.dot(
                pick(main_rows, groups, 0, 1), line, preferred_element_type=F32
            ).astype(BF16)

    def store(dst, first, chunk):
        dims = (((1,), (1,)), ((), ()))
        value = (
            lax.dot_general(dg_ref[...], wg_ref[...], dims, preferred_element_type=F32)
            + lax.dot_general(du_ref[...], wu_ref[...], dims, preferred_element_type=F32)
        ).astype(BF16)
        dst[:, first : first + span] = value[:main_rows]
        for j in range(pieces):
            q = chunk * pieces + j
            stack_ref[q * groups : (q + 1) * groups, :] = value[
                main_rows:, j * piece : (j + 1) * piece
            ]

    for chunk in range(halves):

        @pl.when(step == steps + chunk)
        def _(chunk=chunk):
            store(keep_ref, chunk * span, chunk)
            keep_out(chunk).start()
            if chunk == halves - 1:
                scatter_extra(keep_ref, half)
                keep_out(halves).start()

        @pl.when(step == steps + halves + chunk)
        def _(chunk=chunk):
            if chunk < halves - 1:
                store(away_ref, chunk * span, chunk)
                away_out(chunk).start()
            else:
                store(last_ref, 0, chunk)
                scatter_extra(last_ref, span)
                last_out().start()
                for number in range(halves + 1):
                    keep_out(number).wait()
                for number in range(halves - 1):
                    away_out(number).wait()
                last_out().wait()


def expert_call(cap, head, own, other, w_gate, w_up, head_map, before, after):
    main_rows = own.shape[0]
    width, hidden = w_gate.shape
    half = width // 2
    lanes = half + half // MAIN
    span = 1024
    steps = width // span
    rows = main_rows + main_rows // MAIN
    last_lanes = span + lanes - half + (0 if cap is None else LANES)

    def weight_at(i, head_ref):
        return (lax.rem(head_ref[0] * (steps // 2) + lax.rem(i, steps), steps), 0)

    fixed = lambda i, head_ref: (0, 0)
    anywhere = pl.BlockSpec(memory_space=pl.ANY)
    return pl.pallas_call(
        functools.partial(expert_kernel, span, steps, cap),
        grid_spec=pltpu.PrefetchScalarGridSpec(
            num_scalar_prefetch=1,
            grid=(2 * steps,),
            in_specs=[
                anywhere,
                anywhere,
                pl.BlockSpec((span, hidden), weight_at),
                pl.BlockSpec((span, hidden), weight_at),
                pl.BlockSpec((1, hidden), fixed),
                pl.BlockSpec(before.shape, fixed),
                anywhere,
            ],
            out_specs=[
                anywhere,
                anywhere,
                anywhere,
                pl.BlockSpec((main_rows // MAIN, LANES), fixed),
            ],
            scratch_shapes=[
                pltpu.VMEM((main_rows, lanes), BF16),
                pltpu.VMEM((main_rows, lanes), BF16),
                pltpu.VMEM((main_rows, lanes), BF16),
                pltpu.VMEM((main_rows, half - span), BF16),
                pltpu.VMEM((main_rows, last_lanes), BF16),
                pltpu.VMEM((rows, span), BF16),
                pltpu.VMEM((rows, hidden), F32),
                pltpu.VMEM((rows, hidden), F32),
                pltpu.VMEM((rows, hidden), BF16),
                pltpu.VMEM((rows, hidden), BF16),
                pltpu.VMEM((rows, 1), F32),
                pltpu.VMEM((main_rows, half // MAIN), BF16),
                pltpu.SemaphoreType.DMA((steps // 2 + 2,)),
                pltpu.SemaphoreType.DMA((steps + 2,)),
            ],
        ),
        out_shape=[
            jax.ShapeDtypeStruct((main_rows, lanes), BF16),
            jax.ShapeDtypeStruct((main_rows, half - span), BF16),
            jax.ShapeDtypeStruct((main_rows, last_lanes), BF16),
            jax.ShapeDtypeStruct((main_rows // MAIN, LANES), F32),
        ],
        compiler_params=pltpu.CompilerParams(
            dimension_semantics=("arbitrary",), vmem_limit_bytes=60 << 20
        ),
        cost_estimate=pl.CostEstimate(
            flops=8 * rows * width * hidden,
            bytes_accessed=8 * width * hidden + 8 * main_rows * lanes,
            transcendentals=rows * hidden,
        ),
    )(head, own, other, w_gate, w_up, head_map, before, after)


def first_rows_kernel(head_ref, ids_ref, tok_ref, out_ref, slot_ref, buf_ref, sem):
    toks, half = tok_ref.shape
    experts = slot_ref.shape[0]
    rows = out_ref.shape[0]
    piece = half // MAIN
    numbers = lax.broadcasted_iota(jnp.int32, (experts, toks), 0)
    hits = jnp.zeros((experts, toks), F32)
    for k in range(ids_ref.shape[0]):
        hits = jnp.where(ids_ref[k : k + 1, :] == numbers, 1.0, hits)
    a = lax.broadcasted_iota(jnp.int32, (toks, toks), 0)
    b = lax.broadcasted_iota(jnp.int32, (toks, toks), 1)
    before = jnp.dot(hits.astype(BF16), (a < b).astype(BF16), preferred_element_type=F32)
    slot = jnp.where(hits > 0.0, before, -1.0)
    slot_ref[...] = slot
    a = lax.broadcasted_iota(jnp.int32, (rows, experts), 0)
    b = lax.broadcasted_iota(jnp.int32, (rows, experts), 1)
    spread = ((a >= b * MAIN) & (a < b * MAIN + MAIN)).astype(BF16)
    slot_rows = jnp.dot(spread, slot.astype(BF16), preferred_element_type=F32)
    place = lax.broadcasted_iota(jnp.int32, (rows, toks), 0) % MAIN
    main = (slot_rows == place.astype(F32)).astype(BF16)
    in_extra = slot_rows == float(2 * MAIN)
    extra = 0.0
    copies = []
    for q in range(MAIN + 1):
        cols = slice(q * piece, (q + 1) * piece)
        if q < MAIN:
            buf_ref[:, cols] = jnp.dot(
                main, tok_ref[:, cols], preferred_element_type=F32
            ).astype(BF16)
            here = (in_extra & (place == q)).astype(BF16)
            extra = extra + jnp.dot(here, tok_ref[:, cols], preferred_element_type=F32)
        else:
            buf_ref[:, cols] = extra.astype(BF16)
        copies.append(pltpu.make_async_copy(buf_ref.at[:, cols], out_ref.at[:, cols], sem.at[q]))
        copies[-1].start()
    for copy in copies:
        copy.wait()


def first_rows(head, ids, tokens, experts):
    toks, width = tokens.shape
    half = width // 2
    rows = experts * MAIN
    lanes = half + half // MAIN
    whole = lambda i, head_ref: (0, 0)
    return pl.pallas_call(
        first_rows_kernel,
        grid_spec=pltpu.PrefetchScalarGridSpec(
            num_scalar_prefetch=1,
            grid=(1,),
            in_specs=[
                pl.BlockSpec(ids.shape, whole),
                pl.BlockSpec((toks, half), lambda i, head_ref: (0, head_ref[0])),
            ],
            out_specs=[
                pl.BlockSpec(memory_space=pl.ANY),
                pl.BlockSpec((experts, toks), whole),
            ],
            scratch_shapes=[
                pltpu.VMEM((rows, lanes), BF16),
                pltpu.SemaphoreType.DMA((MAIN + 1,)),
            ],
        ),
        out_shape=[
            jax.ShapeDtypeStruct((rows, lanes), BF16),
            jax.ShapeDtypeStruct((experts, toks), F32),
        ],
        compiler_params=pltpu.CompilerParams(vmem_limit_bytes=60 << 20),
    )(head, ids, tokens)


def join_start(keep_ref, back_ref, last_ref, bufs, sems):
    keep_buf, back_buf, _ = bufs
    chunks, rows, lanes = keep_buf.shape
    cut = back_ref.shape[1]
    arrivals = []
    for i in range(chunks):
        here = slice(i * rows, (i + 1) * rows)
        three = (
            pltpu.make_async_copy(keep_ref.at[here, :], keep_buf.at[i], sems.at[0, i]),
            pltpu.make_async_copy(back_ref.at[here, :], back_buf.at[i, :, :cut], sems.at[1, i]),
            pltpu.make_async_copy(
                last_ref.at[here, : lanes - cut], back_buf.at[i, :, cut:], sems.at[3, i]
            ),
        )
        for copy in three:
            copy.start()
        arrivals.append(three)
    return arrivals


def join_finish(arrivals, out_ref, bufs, sems):
    keep_buf, back_buf, out_buf = bufs
    rows, lanes = keep_buf.shape[1:]
    leaving = []
    for i, three in enumerate(arrivals):
        for copy in three:
            copy.wait()
        out_buf[i] = (keep_buf[i].astype(F32) + back_buf[i].astype(F32)).astype(BF16)
        dst = out_ref.at[i * rows : (i + 1) * rows, :lanes]
        leaving.append(pltpu.make_async_copy(out_buf.at[i], dst, sems.at[2, i]))
        leaving[-1].start()
    for copy in leaving:
        copy.wait()


def join_kernel(keep_ref, back_ref, last_ref, out_ref, keep_buf, back_buf, out_buf, sems):
    bufs = (keep_buf, back_buf, out_buf)
    join_finish(join_start(keep_ref, back_ref, last_ref, bufs, sems), out_ref, bufs, sems)


def join_scratch(rows, lanes):
    chunks = 4
    buf = pltpu.VMEM((chunks, rows // chunks, lanes), BF16)
    return [buf, buf, buf, pltpu.SemaphoreType.DMA((4, chunks))]


def join(keep, back, last):
    anywhere = pl.BlockSpec(memory_space=pl.ANY)
    return pl.pallas_call(
        join_kernel,
        in_specs=[anywhere] * 3,
        out_specs=anywhere,
        out_shape=jax.ShapeDtypeStruct(keep.shape, BF16),
        scratch_shapes=join_scratch(*keep.shape),
        compiler_params=pltpu.CompilerParams(vmem_limit_bytes=60 << 20),
    )(keep, back, last)


def side_kernel(
    cap,
    keep_ref,
    back_ref,
    last_ref,
    own_ref,
    base_ref,
    recv_ref,
    out_ref,
    keep_buf,
    back_buf,
    out_buf,
    sems,
    side_ref,
    other_ref,
    given_ref,
    side_sems,
):
    bufs = (keep_buf, back_buf, out_buf)
    lanes = keep_ref.shape[1]
    first = lanes - back_ref.shape[1]
    arrive = pltpu.make_async_copy(last_ref.at[:, first:], other_ref, side_sems.at[0])
    arrive.start()
    given = pltpu.make_async_copy(recv_ref.at[:, lanes:], given_ref, side_sems.at[2])
    given.start()
    arrivals = join_start(keep_ref, back_ref, last_ref, bufs, sems)
    groups = own_ref.shape[0]
    rows = side_ref.shape[0]
    seqs = base_ref.shape[1]
    lines = seqs // LANES
    seq_dev = seqs // groups
    lane = lax.broadcasted_iota(jnp.int32, (groups, LANES), 1)
    arrive.wait()
    other = jnp.dot(pick(groups, rows, 0, 0), other_ref[...], preferred_element_type=F32)
    scores = jnp.where(lane < cap, own_ref[...] + join_pieces(other, cap), 0.0)
    given.wait()
    side_in = jnp.dot(pick(groups, rows, 0, 0), given_ref[...], preferred_element_type=F32)
    weight = join_pieces(side_in, cap)
    seq_in = pltpu.roll(side_in, LANES - 3 * cap, 1)
    weighted = jnp.where(lane < cap, weight * scores, 0.0)
    a = lax.broadcasted_iota(jnp.int32, (groups, seqs), 0)
    b = lax.broadcasted_iota(jnp.int32, (groups, seqs), 1)
    table = jnp.zeros((groups, seqs), F32)
    for j in range(seq_dev):
        part = jnp.sum(jnp.where(seq_in == float(j), weighted, 0.0), axis=1, keepdims=True)
        table = jnp.where(b == a * seq_dev + j, part, table)
    reward = jnp.sum(table, axis=0, keepdims=True) + base_ref[...]
    place = lax.broadcasted_iota(jnp.int32, (rows, LANES), 0) % MAIN
    side = jnp.zeros((rows, LANES), F32)
    for i, piece in enumerate(pieces_of(reward)):
        for line in range(lines):
            values = piece[:, line * LANES : (line + 1) * LANES].astype(F32)
            side = jnp.where(place == i * lines + line, values, side)
    score_line = spread_pieces(scores, cap)
    chosen = pick(rows, groups, 3 * lines, 1)
    side = side + jnp.dot(chosen, score_line, preferred_element_type=F32)
    side_ref[...] = side.astype(BF16)
    copy = pltpu.make_async_copy(side_ref, out_ref.at[:, lanes:], side_sems.at[1])
    copy.start()
    join_finish(arrivals, out_ref, bufs, sems)
    copy.wait()


def join_with_side(cap, keep, back, last, scores, base, recv):
    rows, lanes = keep.shape
    anywhere = pl.BlockSpec(memory_space=pl.ANY)
    return pl.pallas_call(
        functools.partial(side_kernel, cap),
        out_shape=jax.ShapeDtypeStruct((rows, lanes + LANES), BF16),
        in_specs=[anywhere] * 3 + [pl.BlockSpec()] * 2 + [anywhere],
        out_specs=anywhere,
        scratch_shapes=[
            *join_scratch(rows, lanes),
            pltpu.VMEM((rows, LANES), BF16),
            pltpu.VMEM((rows, LANES), BF16),
            pltpu.VMEM((rows, LANES), BF16),
            pltpu.SemaphoreType.DMA((3,)),
        ],
        compiler_params=pltpu.CompilerParams(vmem_limit_bytes=60 << 20),
    )(keep, back, last, scores, base, recv)


def combiner(home_ref, slot_te, prob_te, first, extra_slot):
    rows = home_ref.shape[0]
    toks, experts = slot_te.shape
    half = home_ref.shape[1] // (LANES * (MAIN + 1)) * LANES * MAIN
    piece = half // MAIN
    a = lax.broadcasted_iota(jnp.int32, (experts, rows), 0)
    b = lax.broadcasted_iota(jnp.int32, (experts, rows), 1)
    spread = ((b >= a * MAIN) & (b < a * MAIN + MAIN)).astype(BF16)
    column = lax.broadcasted_iota(jnp.int32, (toks, rows), 1) % MAIN

    def repeat(x):
        return jnp.dot(x.astype(BF16), spread, preferred_element_type=F32)

    slot = repeat(slot_te)
    high = prob_te.astype(BF16)
    parts = (repeat(high), repeat(prob_te - high.astype(F32)))
    in_main = slot == (column + first).astype(F32)
    in_extra = slot == float(extra_slot)
    main = [jnp.where(in_main, p, 0.0).astype(BF16) for p in parts]

    def block(index):
        lo = index * 2 * piece
        rows_main = home_ref[:, lo : lo + 2 * piece]
        out = sum(jnp.dot(m, rows_main, preferred_element_type=F32) for m in main)
        extra = home_ref[:, half : half + piece]
        sides = []
        for q in (2 * index, 2 * index + 1):
            here = in_extra & (column == q)
            sides.append(
                sum(
                    jnp.dot(
                        jnp.where(here, p, 0.0).astype(BF16), extra, preferred_element_type=F32
                    )
                    for p in parts
                )
            )
        return out + jnp.concatenate(sides, axis=1)

    return block, 2 * piece


def first_combine_kernel(home_ref, slot_ref, prob_ref, line_ref, out_ref):
    block, width = combiner(home_ref, slot_ref[...], prob_ref[...], 0, 2 * MAIN)
    for i in range(out_ref.shape[1] // width):
        cols = slice(i * width, (i + 1) * width)
        out_ref[:, cols] = block(i) + line_ref[:, cols]


def fit_line(values, seq_lengths):
    n = float(values.shape[1])
    s1 = jnp.sum(seq_lengths, axis=1, keepdims=True)
    s2 = jnp.sum(seq_lengths * seq_lengths, axis=1, keepdims=True)
    v0 = jnp.sum(values, axis=1, keepdims=True)
    v1 = jnp.sum(values * seq_lengths, axis=1, keepdims=True)
    slope = (n * v1 - s1 * v0) / (n * s2 - s1 * s1)
    offset = (v0 - slope * s1) / n
    return values - offset - slope * seq_lengths


def last_combine_kernel(
    cap,
    home_ref,
    slot_ref,
    prob_ref,
    slot_et_ref,
    prob_et_ref,
    acc_ref,
    router_ref,
    lens_ref,
    pairs_ref,
    member_ref,
    out_ref,
):
    rows = home_ref.shape[0]
    experts = rows // MAIN
    seqs = lens_ref.shape[1]
    lines = seqs // LANES
    side = home_ref[:, home_ref.shape[1] - LANES :]
    chosen = pick(experts, rows, 3 * lines, 0)
    packed = jnp.dot(chosen, side, preferred_element_type=F32)
    score_es = join_pieces(packed, cap)
    slot_et = slot_et_ref[...]
    prob_et = prob_et_ref[...]
    score_et = jnp.zeros_like(prob_et)
    for c, number in enumerate(slot_order()):
        score_et = score_et + jnp.where(slot_et == float(number), score_es[:, c : c + 1], 0.0)
    mean_score = jnp.sum(prob_et * score_et, axis=0, keepdims=True)
    dlogits = (prob_et * (score_et - mean_score)).astype(BF16)
    totals = jnp.sum(side.astype(F32).reshape(experts, MAIN, LANES), axis=0)
    totals = totals[:lines] + totals[lines : 2 * lines] + totals[2 * lines : 3 * lines]
    reward = jnp.concatenate([totals[i : i + 1] for i in range(lines)], axis=1)
    lens = lens_ref[...]
    residual = fit_line(reward, lens)
    numbers = lax.broadcasted_iota(jnp.int32, (pairs_ref.shape[0], seqs), 1)
    delta = (numbers == pairs_ref[:, 0:1]).astype(F32) - (numbers == pairs_ref[:, 1:2]).astype(F32)
    margin = jnp.sum(delta * residual, axis=1, keepdims=True)
    pull = LOSS_SCALE / (1.0 + jnp.exp(margin))
    reward_grad = -jnp.sum(pull * delta, axis=0, keepdims=True)
    grad_back = fit_line(reward_grad, lens)
    coef = jnp.sum(member_ref[...] * grad_back, axis=1, keepdims=True)

    block, width = combiner(home_ref, slot_ref[...], prob_ref[...], MAIN, 2 * MAIN + 1)
    for i in range(out_ref.shape[1] // width):
        cols = slice(i * width, (i + 1) * width)
        router_term = lax.dot_general(
            dlogits, router_ref[:, cols], (((0,), (0,)), ((), ())), preferred_element_type=F32
        )
        out_ref[:, cols] = (coef * (block(i) + acc_ref[:, cols] + router_term)).astype(BF16)


def expand(extra_mask, pieces):
    experts, toks = extra_mask.shape
    eye = jnp.eye(pieces, dtype=extra_mask.dtype)
    full = extra_mask[:, None, None, :] * eye[None, :, :, None]
    return full.reshape(experts * pieces, pieces * toks)


def per_device(
    tokens,
    router_weight,
    gate_weight,
    up_weight,
    down_weight,
    head_weight,
    expert_ids,
    lengths,
    pairs,
):
    toks, width = tokens.shape
    experts = router_weight.shape[1]
    groups = lengths.shape[0]
    seq_dev = lengths.shape[1]
    seqs = groups * seq_dev
    half = width // 2
    piece = half // MAIN
    cap = 2 * (MAIN + 1)
    me = lax.axis_index("expert")
    head = lax.axis_index("head")
    w_gate, w_up, w_down = gate_weight[0], up_weight[0], down_weight[0]

    main_rows = groups * MAIN
    head_number = head.astype(jnp.int32)[None]
    block_a, slot_ef = first_rows(head_number, expert_ids.T, tokens, experts)
    slot_te = slot_ef.T
    recv_a = exchange(block_a.reshape(experts, MAIN, -1))
    hits = slot_te >= 0.0
    slot_et = slot_ef.astype(jnp.int32)

    def masks(first, extra):
        slots = first + jnp.arange(MAIN, dtype=jnp.int32)
        main = (slot_et[:, None, :] == slots[None, :, None]).astype(BF16)
        return main.reshape(experts * MAIN, toks), (slot_et == extra).astype(BF16)

    mask_b = masks(MAIN, 2 * MAIN + 1)
    tok_half = lax.dynamic_slice_in_dim(tokens, head * half, half, 1)
    tok_pieces = tok_half.reshape(toks, MAIN, piece).transpose(1, 0, 2).reshape(MAIN * toks, piece)

    def gather_rows(mask):
        main = jnp.dot(mask[0], tok_half, preferred_element_type=F32).astype(BF16)
        extra = jnp.dot(expand(mask[1], MAIN), tok_pieces, preferred_element_type=F32).astype(BF16)
        return jnp.concatenate(
            [main.reshape(experts, MAIN, half), extra.reshape(experts, MAIN, piece)], axis=2
        )


    logits = jnp.dot(tokens, router_weight, preferred_element_type=F32)
    masked = jnp.where(hits, logits, -jnp.inf)
    top = jnp.max(masked, axis=1, keepdims=True)
    weights = jnp.where(hits, jnp.exp(logits - top), 0.0)
    prob = weights / jnp.sum(weights, axis=1, keepdims=True)
    own_lengths = lax.dynamic_slice_in_dim(lengths, me, 1, 0)[0]
    ends = jnp.cumsum(own_lengths)
    starts = ends - own_lengths
    position = jnp.arange(toks, dtype=jnp.int32)[:, None]
    member = ((position >= starts[None, :]) & (position < ends[None, :])).astype(F32)
    own_float = own_lengths.astype(F32)
    seq_of = jnp.sum(member * jnp.arange(seq_dev, dtype=F32)[None, :], axis=1)
    inv_len = jnp.sum(member / own_float[None, :], axis=1)

    slot_iota = jnp.array(slot_order(), jnp.int32)
    at_slot = slot_et[:, None, :] == slot_iota[None, :, None]
    weight_et = (prob * inv_len[:, None]).T
    weight_slot = jnp.sum(jnp.where(at_slot, weight_et[:, None, :], 0.0), axis=2)
    seq_slot = jnp.sum(jnp.where(at_slot, seq_of[None, None, :], 0.0), axis=2)
    side = jnp.concatenate([*split_three(weight_slot), seq_slot.astype(BF16)], axis=1)
    side = jnp.pad(side, ((0, 0), (0, LANES - 4 * cap)))
    side = jnp.pad(side[:, None, :], ((0, 0), (0, MAIN - 1), (0, 0)))
    block_b = jnp.concatenate([gather_rows(mask_b), side], axis=2)
    recv_b = exchange(block_b)

    head_map = jnp.dot(w_down, head_weight, preferred_element_type=F32)
    base = jnp.dot(tokens, head_weight, preferred_element_type=F32)
    base_reward = jnp.sum(base[:, None] * member, axis=0) / own_float

    head_line = head_map[None, :]

    def work(cap, recv, other, before, after):
        own = recv.reshape(main_rows, -1)
        return expert_call(
            cap,
            head_number,
            own,
            other.reshape(main_rows, -1),
            w_gate,
            w_up,
            head_line,
            before,
            after,
        )

    own_row = jnp.arange(groups, dtype=jnp.int32)[:, None] == me
    base_line = jnp.where(own_row, base_reward[None, :], 0.0).reshape(1, seqs)
    recv_a = touch(recv_a, block_b, head_line, base_line)
    keep_a, away_a, last_a, score_a = work(None, recv_a, swap(recv_a), head_line, head_line)
    total_a = join(keep_a, swap(away_a), swap(last_a)).reshape(groups, MAIN, -1)
    recv_b = touch(recv_b, total_a)
    keep_b, away_b, last_b, score_b = work(cap, recv_b, swap(recv_b), score_a, total_a)
    home_a = exchange(total_a)
    total_b = join_with_side(
        cap, keep_b, swap(away_b), swap(last_b), score_b, base_line, recv_b.reshape(main_rows, -1)
    )
    total_b = touch(total_b, home_a[0, :, :LANES])
    home_b = exchange(total_b.reshape(groups, MAIN, -1))

    head_half = lax.dynamic_slice_in_dim(head_weight, head * half, half, 0).astype(F32)[None, :]
    acc = pl.pallas_call(
        first_combine_kernel,
        out_shape=jax.ShapeDtypeStruct((toks, half), F32),
        compiler_params=pltpu.CompilerParams(vmem_limit_bytes=60 << 20),
    )(home_a.reshape(main_rows, -1), slot_te, prob, head_half)

    router_half = lax.dynamic_slice_in_dim(router_weight, head * half, half, 0).T
    own_seq = me * seq_dev + jnp.arange(seq_dev, dtype=jnp.int32)
    places = (jnp.arange(seqs, dtype=jnp.int32)[None, :] == own_seq[:, None]).astype(F32)
    member_line = jnp.sum((member / own_float[None, :])[:, :, None] * places[None], axis=1)
    return pl.pallas_call(
        functools.partial(last_combine_kernel, cap),
        out_shape=jax.ShapeDtypeStruct((toks, half), BF16),
        in_specs=[pl.BlockSpec(memory_space=pltpu.VMEM)] + [pl.BlockSpec()] * 9,
        compiler_params=pltpu.CompilerParams(vmem_limit_bytes=24 << 20),
    )(
        home_b.reshape(main_rows, -1),
        slot_te,
        prob,
        slot_ef,
        prob.T,
        acc,
        router_half,
        lengths.astype(F32).reshape(1, seqs),
        pairs,
        member_line,
    )


def solution(mesh):
    return jax.shard_map(
        per_device,
        mesh=mesh,
        in_specs=(
            P("expert", None),
            P(),
            P("expert", None, "head"),
            P("expert", None, "head"),
            P("expert", "head", None),
            P(),
            P("expert", None),
            P(),
            P(),
        ),
        out_specs=P("expert", "head"),
        check_vma=False,
    )
```

```python
import functools

import jax
import jax.numpy as jnp
from jax import lax
from jax.experimental import pallas as pl
from jax.experimental.pallas import tpu as pltpu
from jax.sharding import PartitionSpec as P

LOSS_SCALE = 1024
MAIN = 8
LANES = 128
SWAP = [(0, 1), (1, 0)]
F32 = jnp.float32
BF16 = jnp.bfloat16


def split_three(x):
    high = lax.reduce_precision(x, 8, 7)
    middle = lax.reduce_precision(x - high, 8, 7)
    low = x - high - middle
    return high.astype(BF16), middle.astype(BF16), low.astype(BF16)


def exchange(x):
    return lax.all_to_all(x, "expert", split_axis=0, concat_axis=0, tiled=True)


def swap(x):
    return lax.ppermute(x, "head", SWAP)


def pick(rows, cols, first, axis):
    a = lax.broadcasted_iota(jnp.int32, (rows, cols), axis)
    b = lax.broadcasted_iota(jnp.int32, (rows, cols), 1 - axis)
    return (b == a * MAIN + first).astype(BF16)


def shuffle(rows, groups):
    a = lax.broadcasted_iota(jnp.int32, (rows, rows), 0)
    b = lax.broadcasted_iota(jnp.int32, (rows, rows), 1)
    return (b == (a % groups) * MAIN + a // groups).astype(BF16)


def slot_order():
    return [*range(MAIN), 2 * MAIN, *range(MAIN, 2 * MAIN), 2 * MAIN + 1]


def pieces_of(x):
    high = x.astype(BF16)
    rest = x - high.astype(F32)
    middle = rest.astype(BF16)
    return high, middle, (rest - middle.astype(F32)).astype(BF16)


def spread_pieces(x, cap):
    line = jnp.zeros(x.shape, F32)
    for i, piece in enumerate(pieces_of(x)):
        piece = piece.astype(F32)
        line = line + (pltpu.roll(piece, i * cap, 1) if i else piece)
    return line.astype(BF16)


def join_pieces(line, cap):
    return (
        line + pltpu.roll(line, LANES - cap, 1) + pltpu.roll(line, LANES - 2 * cap, 1)
    )


def touch_kernel(*refs):
    pass


def touch(x, *after):
    return pl.pallas_call(
        touch_kernel,
        out_shape=jax.ShapeDtypeStruct(x.shape, x.dtype),
        in_specs=[pl.BlockSpec(memory_space=pl.ANY)] * (1 + len(after)),
        out_specs=pl.BlockSpec(memory_space=pl.ANY),
        input_output_aliases={0: 0},
    )(x, *after)


def forward_kernel(
    span,
    steps,
    cap,
    head_ref,
    own_hbm,
    other_hbm,
    wg_ref,
    wu_ref,
    hm_ref,
    before_ref,
    after_ref,
    dg_ref,
    du_ref,
    score_ref,
    own_ref,
    other_ref,
    x_ref,
    gate_ref,
    up_ref,
    column_ref,
    stack_ref,
    in_sems,
):
    step = pl.program_id(0)
    main_rows, lanes = own_ref.shape
    groups = main_rows // MAIN
    rows = gate_ref.shape[0]
    halves = steps // 2
    half = halves * span
    piece = half // MAIN
    pieces = span // piece
    own_cols = [slice(i * span, (i + 1) * span) for i in range(halves)] + [slice(half, lanes)]

    def own_in(i):
        cols = own_cols[i]
        return pltpu.make_async_copy(own_hbm.at[:, cols], own_ref.at[:, cols], in_sems.at[i])

    def other_in():
        return pltpu.make_async_copy(other_hbm.at[:, :lanes], other_ref, in_sems.at[halves + 1])

    def gather_extra(src):
        stack_ref[...] = jnp.dot(
            shuffle(main_rows, groups), src[:, half : half + piece], preferred_element_type=F32
        ).astype(BF16)

    def fill(src, chunk):
        x_ref[:main_rows, :] = src[:, chunk * span : (chunk + 1) * span]
        for j in range(pieces):
            q = chunk * pieces + j
            x_ref[main_rows:, j * piece : (j + 1) * piece] = stack_ref[
                q * groups : (q + 1) * groups, :
            ]

    for i in range(steps):

        @pl.when(step == i)
        def _(i=i):
            if i == 0:
                for number in (0, halves, *range(1, halves)):
                    own_in(number).start()
                other_in().start()
                own_in(halves).wait()
                gather_extra(own_ref)
            if i < halves:
                own_in(i).wait()
                fill(own_ref, i)
            else:
                if i == halves:
                    other_in().wait()
                    gather_extra(other_ref)
                fill(other_ref, i - halves)

    @pl.when(step == 0)
    def _():
        gate_ref[...] = jnp.dot(x_ref[...], wg_ref[...], preferred_element_type=F32)
        up_ref[...] = jnp.dot(x_ref[...], wu_ref[...], preferred_element_type=F32)

    @pl.when(step > 0)
    def _():
        gate_ref[...] += jnp.dot(x_ref[...], wg_ref[...], preferred_element_type=F32)
        up_ref[...] += jnp.dot(x_ref[...], wu_ref[...], preferred_element_type=F32)

    @pl.when(step == steps - 1)
    def _():
        block = 64
        head_map = hm_ref[...]

        def body(i, carry):
            here = pl.ds(pl.multiple_of(i * block, block), block)
            gate = gate_ref[here, :]
            up = up_ref[here, :]
            sig = 1.0 / (1.0 + jnp.exp(-gate))
            act = gate * sig
            hidden = (act * up).astype(BF16).astype(F32)
            column_ref[here, :] = jnp.sum(hidden * head_map, axis=1, keepdims=True)
            du_ref[here, :] = (head_map * act).astype(BF16)
            dg_ref[here, :] = (head_map * up * sig * (1.0 + gate * (1.0 - sig))).astype(BF16)
            return carry

        lax.fori_loop(0, rows // block, body, 0)
        place = lax.broadcasted_iota(jnp.int32, (main_rows, LANES), 0) % MAIN
        lane = lax.broadcasted_iota(jnp.int32, (main_rows, LANES), 1)
        table = jnp.where(lane == place, column_ref[:main_rows, :], 0.0)
        a = lax.broadcasted_iota(jnp.int32, (groups, main_rows), 0)
        b = lax.broadcasted_iota(jnp.int32, (groups, main_rows), 1)
        fold = ((b >= a * MAIN) & (b < a * MAIN + MAIN)).astype(BF16)
        folded = sum(jnp.dot(fold, t, preferred_element_type=F32) for t in pieces_of(table))
        lane = lax.broadcasted_iota(jnp.int32, (groups, LANES), 1)
        score = jnp.where(lane == MAIN, column_ref[main_rows:, :], folded)
        if cap is None:
            score_ref[...] = score
        else:
            score = jnp.where(lane <= MAIN, before_ref[...], pltpu.roll(score, MAIN + 1, 1))
            score = jnp.where(lane < cap, score, 0.0)
            score_ref[...] = score
            du_ref[rows:, :] = jnp.zeros((groups, du_ref.shape[1]), BF16)
            du_ref[rows:, :LANES] = spread_pieces(score, cap)


def forward_call(cap, head, own, other, w_gate, w_up, head_map, before, after):
    main_rows = own.shape[0]
    width, hidden = w_gate.shape
    groups = main_rows // MAIN
    half = width // 2
    lanes = half + half // MAIN
    span = 1024
    steps = width // span
    rows = main_rows + groups
    out_rows = rows if cap is None else rows + groups

    def weight_at(i, head_ref):
        return (lax.rem(head_ref[0] * (steps // 2) + i, steps), 0)

    fixed = lambda i, head_ref: (0, 0)
    anywhere = pl.BlockSpec(memory_space=pl.ANY)
    return pl.pallas_call(
        functools.partial(forward_kernel, span, steps, cap),
        grid_spec=pltpu.PrefetchScalarGridSpec(
            num_scalar_prefetch=1,
            grid=(steps,),
            in_specs=[
                anywhere,
                anywhere,
                pl.BlockSpec((span, hidden), weight_at),
                pl.BlockSpec((span, hidden), weight_at),
                pl.BlockSpec((1, hidden), fixed),
                pl.BlockSpec(before.shape, fixed),
                anywhere,
            ],
            out_specs=[
                pl.BlockSpec((rows, hidden), fixed),
                pl.BlockSpec((out_rows, hidden), fixed),
                pl.BlockSpec((groups, LANES), fixed),
            ],
            scratch_shapes=[
                pltpu.VMEM((main_rows, lanes), BF16),
                pltpu.VMEM((main_rows, lanes), BF16),
                pltpu.VMEM((rows, span), BF16),
                pltpu.VMEM((rows, hidden), F32),
                pltpu.VMEM((rows, hidden), F32),
                pltpu.VMEM((rows, 1), F32),
                pltpu.VMEM((main_rows, half // MAIN), BF16),
                pltpu.SemaphoreType.DMA((steps // 2 + 2,)),
            ],
        ),
        out_shape=[
            jax.ShapeDtypeStruct((rows, hidden), BF16),
            jax.ShapeDtypeStruct((out_rows, hidden), BF16),
            jax.ShapeDtypeStruct((groups, LANES), F32),
        ],
        compiler_params=pltpu.CompilerParams(
            dimension_semantics=("arbitrary",), vmem_limit_bytes=62 << 20
        ),
    )(head, own, other, w_gate, w_up, head_map, before, after)


def make_side(cap, own, other, side_in, base, rows):
    groups = own.shape[0]
    seqs = base.shape[1]
    lines = seqs // LANES
    seq_dev = seqs // groups
    lane = lax.broadcasted_iota(jnp.int32, (groups, LANES), 1)
    scores = jnp.where(lane < cap, own + join_pieces(other, cap), 0.0)
    seq_in = pltpu.roll(side_in, LANES - 3 * cap, 1)
    weighted = jnp.where(lane < cap, join_pieces(side_in, cap) * scores, 0.0)
    a = lax.broadcasted_iota(jnp.int32, (groups, seqs), 0)
    b = lax.broadcasted_iota(jnp.int32, (groups, seqs), 1)
    table = jnp.zeros((groups, seqs), F32)
    for j in range(seq_dev):
        part = jnp.sum(jnp.where(seq_in == float(j), weighted, 0.0), axis=1, keepdims=True)
        table = jnp.where(b == a * seq_dev + j, part, table)
    reward = jnp.sum(table, axis=0, keepdims=True) + base
    place = lax.broadcasted_iota(jnp.int32, (rows, LANES), 0) % MAIN
    side = jnp.zeros((rows, LANES), F32)
    for i, piece in enumerate(pieces_of(reward)):
        for line in range(lines):
            values = piece[:, line * LANES : (line + 1) * LANES].astype(F32)
            side = jnp.where(place == i * lines + line, values, side)
    chosen = pick(rows, groups, 3 * lines, 1)
    side = side + jnp.dot(chosen, spread_pieces(scores, cap), preferred_element_type=F32)
    return side.astype(BF16)


def backward_kernel(span, steps, cap, head_ref, *refs):
    if cap is None:
        dg0, du0, dg1, du1, wg0, wu0, wg1, wu1, out_hbm, out_ref, stack_ref, sems = refs
    else:
        (dg0, du0, dg1, du1, wg0, wu0, wg1, wu1, own_ref, base_ref, recv_hbm) = refs[:11]
        out_hbm, out_ref, stack_ref, sems, given_ref = refs[11:]
    step = pl.program_id(0)
    main_rows, lanes = out_ref.shape
    groups = main_rows // MAIN
    rows = dg0.shape[0]
    half = steps * span
    piece = half // MAIN
    pieces = span // piece

    def given():
        return pltpu.make_async_copy(
            recv_hbm.at[:, half + piece :], given_ref, sems.at[steps + 1]
        )

    def leaving(i):
        cols = slice(i * span, (i + 1) * span) if i < steps else slice(half, lanes)
        return pltpu.make_async_copy(out_ref.at[:, cols], out_hbm.at[:, cols], sems.at[i])

    for chunk in range(steps):

        @pl.when(step == chunk)
        def _(chunk=chunk):
            if chunk == 0 and cap is not None:
                given().start()
            dims = (((1,), (1,)), ((), ()))
            value = 0.0
            for grad, weight in ((dg0, wg0), (du0, wu0), (dg1, wg1), (du1, wu1)):
                value = value + lax.dot_general(
                    grad[:rows, :], weight[...], dims, preferred_element_type=F32
                )
            value = value.astype(BF16)
            out_ref[:, chunk * span : (chunk + 1) * span] = value[:main_rows]
            leaving(chunk).start()
            for j in range(pieces):
                q = chunk * pieces + j
                stack_ref[q * groups : (q + 1) * groups, :] = value[
                    main_rows:, j * piece : (j + 1) * piece
                ]
            if chunk == steps - 1:
                out_ref[:, half : half + piece] = lax.dot_general(
                    shuffle(main_rows, groups),
                    stack_ref[...],
                    (((0,), (0,)), ((), ())),
                    preferred_element_type=F32,
                ).astype(BF16)
                if cap is not None:
                    given().wait()
                    side_in = jnp.dot(
                        pick(groups, main_rows, 0, 0), given_ref[...], preferred_element_type=F32
                    )
                    out_ref[:, half + piece :] = make_side(
                        cap,
                        own_ref[...],
                        du1[rows:, :LANES].astype(F32),
                        side_in,
                        base_ref[...],
                        main_rows,
                    )
                leaving(steps).start()
                for number in range(steps + 1):
                    leaving(number).wait()


def backward_call(cap, head, grads, weights, crossed, *side):
    dg = grads[0]
    hidden = dg.shape[1]
    half = weights[0].shape[0] // 2
    span = 512
    steps = half // span
    rows = dg.shape[0]
    main_rows = rows // (MAIN + 1) * MAIN
    lanes = half + half // MAIN + (0 if cap is None else LANES)
    fixed = lambda i, head_ref: (0, 0)
    here = lambda i, head_ref: (head_ref[0] * steps + i, 0)
    anywhere = pl.BlockSpec(memory_space=pl.ANY)
    side_specs = [pl.BlockSpec(x.shape, fixed) for x in side[:-1]] + [anywhere] * len(side[-1:])
    side_scratch = [] if cap is None else [pltpu.VMEM((main_rows, LANES), BF16)]
    return pl.pallas_call(
        functools.partial(backward_kernel, span, steps, cap),
        grid_spec=pltpu.PrefetchScalarGridSpec(
            num_scalar_prefetch=1,
            grid=(steps,),
            in_specs=[pl.BlockSpec(x.shape, fixed) for x in grads]
            + [pl.BlockSpec((span, hidden), here)] * 4
            + side_specs,
            out_specs=anywhere,
            scratch_shapes=[
                pltpu.VMEM((main_rows, lanes), BF16),
                pltpu.VMEM((main_rows, half // MAIN), BF16),
                pltpu.SemaphoreType.DMA((steps + 2,)),
                *side_scratch,
            ],
        ),
        out_shape=jax.ShapeDtypeStruct((main_rows, lanes), BF16),
        compiler_params=pltpu.CompilerParams(
            dimension_semantics=("arbitrary",), vmem_limit_bytes=62 << 20
        ),
    )(head, *grads, *weights, *crossed, *side)


def first_rows_kernel(head_ref, ids_ref, tok_ref, out_ref, slot_ref, buf_ref, stack_ref, sem):
    toks, half = tok_ref.shape
    experts = slot_ref.shape[0]
    rows = out_ref.shape[0]
    piece = half // MAIN
    numbers = lax.broadcasted_iota(jnp.int32, (experts, toks), 0)
    hits = jnp.zeros((experts, toks), F32)
    for k in range(ids_ref.shape[0]):
        hits = jnp.where(ids_ref[k : k + 1, :] == numbers, 1.0, hits)
    a = lax.broadcasted_iota(jnp.int32, (toks, toks), 0)
    b = lax.broadcasted_iota(jnp.int32, (toks, toks), 1)
    before = jnp.dot(hits.astype(BF16), (a < b).astype(BF16), preferred_element_type=F32)
    slot = jnp.where(hits > 0.0, before, -1.0)
    slot_ref[...] = slot
    a = lax.broadcasted_iota(jnp.int32, (rows, experts), 0)
    b = lax.broadcasted_iota(jnp.int32, (rows, experts), 1)
    spread = ((a >= b * MAIN) & (a < b * MAIN + MAIN)).astype(BF16)
    slot_rows = jnp.dot(spread, slot.astype(BF16), preferred_element_type=F32)
    place = lax.broadcasted_iota(jnp.int32, (rows, toks), 0) % MAIN
    main = (slot_rows == place.astype(F32)).astype(BF16)
    in_extra = (slot == float(2 * MAIN)).astype(BF16)
    copies = []
    for q in range(MAIN + 1):
        cols = slice(q * piece, (q + 1) * piece)
        if q < MAIN:
            buf_ref[:, cols] = jnp.dot(
                main, tok_ref[:, cols], preferred_element_type=F32
            ).astype(BF16)
            stack_ref[q * experts : (q + 1) * experts, :] = jnp.dot(
                in_extra, tok_ref[:, cols], preferred_element_type=F32
            ).astype(BF16)
        else:
            dims = (((0,), (0,)), ((), ()))
            buf_ref[:, cols] = lax.dot_general(
                shuffle(rows, experts), stack_ref[...], dims, preferred_element_type=F32
            ).astype(BF16)
        copies.append(pltpu.make_async_copy(buf_ref.at[:, cols], out_ref.at[:, cols], sem.at[q]))
        copies[-1].start()
    for copy in copies:
        copy.wait()


def first_rows(head, ids, tokens, experts):
    toks, width = tokens.shape
    half = width // 2
    rows = experts * MAIN
    lanes = half + half // MAIN
    whole = lambda i, head_ref: (0, 0)
    return pl.pallas_call(
        first_rows_kernel,
        grid_spec=pltpu.PrefetchScalarGridSpec(
            num_scalar_prefetch=1,
            grid=(1,),
            in_specs=[
                pl.BlockSpec(ids.shape, whole),
                pl.BlockSpec((toks, half), lambda i, head_ref: (0, head_ref[0])),
            ],
            out_specs=[
                pl.BlockSpec(memory_space=pl.ANY),
                pl.BlockSpec((experts, toks), whole),
            ],
            scratch_shapes=[
                pltpu.VMEM((rows, lanes), BF16),
                pltpu.VMEM((rows, half // MAIN), BF16),
                pltpu.SemaphoreType.DMA((MAIN + 1,)),
            ],
        ),
        out_shape=[
            jax.ShapeDtypeStruct((rows, lanes), BF16),
            jax.ShapeDtypeStruct((experts, toks), F32),
        ],
        compiler_params=pltpu.CompilerParams(vmem_limit_bytes=60 << 20),
    )(head, ids, tokens)


def combiner(home_ref, slot_te, prob_te, first, extra_slot):
    rows = home_ref.shape[0]
    toks, experts = slot_te.shape
    half = home_ref.shape[1] // (LANES * (MAIN + 1)) * LANES * MAIN
    piece = half // MAIN
    a = lax.broadcasted_iota(jnp.int32, (experts, rows), 0)
    b = lax.broadcasted_iota(jnp.int32, (experts, rows), 1)
    spread = ((b >= a * MAIN) & (b < a * MAIN + MAIN)).astype(BF16)
    column = lax.broadcasted_iota(jnp.int32, (toks, rows), 1) % MAIN

    def repeat(x):
        return jnp.dot(x.astype(BF16), spread, preferred_element_type=F32)

    slot = repeat(slot_te)
    high = prob_te.astype(BF16)
    parts = (repeat(high), repeat(prob_te - high.astype(F32)))
    in_main = slot == (column + first).astype(F32)
    in_extra = slot == float(extra_slot)
    main = [jnp.where(in_main, p, 0.0).astype(BF16) for p in parts]

    def block(index):
        lo = index * 2 * piece
        rows_main = home_ref[:, lo : lo + 2 * piece]
        out = sum(jnp.dot(m, rows_main, preferred_element_type=F32) for m in main)
        extra = home_ref[:, half : half + piece]
        sides = []
        for q in (2 * index, 2 * index + 1):
            here = in_extra & (column == q)
            sides.append(
                sum(
                    jnp.dot(
                        jnp.where(here, p, 0.0).astype(BF16), extra, preferred_element_type=F32
                    )
                    for p in parts
                )
            )
        return out + jnp.concatenate(sides, axis=1)

    return block, 2 * piece


def first_combine_kernel(home_ref, slot_ref, prob_ref, line_ref, out_ref):
    block, width = combiner(home_ref, slot_ref[...], prob_ref[...], 0, 2 * MAIN)
    for i in range(out_ref.shape[1] // width):
        cols = slice(i * width, (i + 1) * width)
        out_ref[:, cols] = block(i) + line_ref[:, cols]


def fit_line(values, seq_lengths):
    n = float(values.shape[1])
    s1 = jnp.sum(seq_lengths, axis=1, keepdims=True)
    s2 = jnp.sum(seq_lengths * seq_lengths, axis=1, keepdims=True)
    v0 = jnp.sum(values, axis=1, keepdims=True)
    v1 = jnp.sum(values * seq_lengths, axis=1, keepdims=True)
    slope = (n * v1 - s1 * v0) / (n * s2 - s1 * s1)
    offset = (v0 - slope * s1) / n
    return values - offset - slope * seq_lengths


def last_combine_kernel(
    cap,
    home_ref,
    slot_ref,
    prob_ref,
    slot_et_ref,
    prob_et_ref,
    acc_ref,
    router_ref,
    lens_ref,
    pairs_ref,
    member_ref,
    out_ref,
):
    rows = home_ref.shape[0]
    experts = rows // MAIN
    seqs = lens_ref.shape[1]
    lines = seqs // LANES
    side = home_ref[:, home_ref.shape[1] - LANES :]
    chosen = pick(experts, rows, 3 * lines, 0)
    packed = jnp.dot(chosen, side, preferred_element_type=F32)
    score_es = join_pieces(packed, cap)
    slot_et = slot_et_ref[...]
    prob_et = prob_et_ref[...]
    score_et = jnp.zeros_like(prob_et)
    for c, number in enumerate(slot_order()):
        score_et = score_et + jnp.where(slot_et == float(number), score_es[:, c : c + 1], 0.0)
    mean_score = jnp.sum(prob_et * score_et, axis=0, keepdims=True)
    dlogits = (prob_et * (score_et - mean_score)).astype(BF16)
    totals = jnp.sum(side.astype(F32).reshape(experts, MAIN, LANES), axis=0)
    totals = totals[:lines] + totals[lines : 2 * lines] + totals[2 * lines : 3 * lines]
    reward = jnp.concatenate([totals[i : i + 1] for i in range(lines)], axis=1)
    lens = lens_ref[...]
    residual = fit_line(reward, lens)
    numbers = lax.broadcasted_iota(jnp.int32, (pairs_ref.shape[0], seqs), 1)
    delta = (numbers == pairs_ref[:, 0:1]).astype(F32) - (numbers == pairs_ref[:, 1:2]).astype(F32)
    margin = jnp.sum(delta * residual, axis=1, keepdims=True)
    pull = LOSS_SCALE / (1.0 + jnp.exp(margin))
    reward_grad = -jnp.sum(pull * delta, axis=0, keepdims=True)
    grad_back = fit_line(reward_grad, lens)
    coef = jnp.sum(member_ref[...] * grad_back, axis=1, keepdims=True)

    block, width = combiner(home_ref, slot_ref[...], prob_ref[...], MAIN, 2 * MAIN + 1)
    for i in range(out_ref.shape[1] // width):
        cols = slice(i * width, (i + 1) * width)
        router_term = lax.dot_general(
            dlogits, router_ref[:, cols], (((0,), (0,)), ((), ())), preferred_element_type=F32
        )
        out_ref[:, cols] = (coef * (block(i) + acc_ref[:, cols] + router_term)).astype(BF16)


def expand(extra_mask, pieces):
    experts, toks = extra_mask.shape
    eye = jnp.eye(pieces, dtype=extra_mask.dtype)
    full = extra_mask[:, None, None, :] * eye[None, :, :, None]
    return full.reshape(experts * pieces, pieces * toks)


def per_device(
    tokens,
    router_weight,
    gate_weight,
    up_weight,
    down_weight,
    head_weight,
    expert_ids,
    lengths,
    pairs,
):
    toks, width = tokens.shape
    experts = router_weight.shape[1]
    groups = lengths.shape[0]
    seq_dev = lengths.shape[1]
    seqs = groups * seq_dev
    half = width // 2
    piece = half // MAIN
    cap = 2 * (MAIN + 1)
    me = lax.axis_index("expert")
    head = lax.axis_index("head")
    w_gate, w_up, w_down = gate_weight[0], up_weight[0], down_weight[0]

    main_rows = groups * MAIN
    head_number = head.astype(jnp.int32)[None]
    block_a, slot_ef = first_rows(head_number, expert_ids.T, tokens, experts)
    slot_te = slot_ef.T
    recv_a = exchange(block_a.reshape(experts, MAIN, -1))
    hits = slot_te >= 0.0
    slot_et = slot_ef.astype(jnp.int32)

    def masks(first, extra):
        slots = first + jnp.arange(MAIN, dtype=jnp.int32)
        main = (slot_et[:, None, :] == slots[None, :, None]).astype(BF16)
        return main.reshape(experts * MAIN, toks), (slot_et == extra).astype(BF16)

    mask_b = masks(MAIN, 2 * MAIN + 1)
    tok_half = lax.dynamic_slice_in_dim(tokens, head * half, half, 1)
    tok_pieces = tok_half.reshape(toks, MAIN, piece).transpose(1, 0, 2).reshape(MAIN * toks, piece)

    def gather_rows(mask):
        main = jnp.dot(mask[0], tok_half, preferred_element_type=F32).astype(BF16)
        extra = jnp.dot(expand(mask[1], MAIN), tok_pieces, preferred_element_type=F32).astype(BF16)
        return jnp.concatenate(
            [main.reshape(experts, MAIN, half), extra.reshape(experts, MAIN, piece)], axis=2
        )


    logits = jnp.dot(tokens, router_weight, preferred_element_type=F32)
    masked = jnp.where(hits, logits, -jnp.inf)
    top = jnp.max(masked, axis=1, keepdims=True)
    weights = jnp.where(hits, jnp.exp(logits - top), 0.0)
    prob = weights / jnp.sum(weights, axis=1, keepdims=True)
    own_lengths = lax.dynamic_slice_in_dim(lengths, me, 1, 0)[0]
    ends = jnp.cumsum(own_lengths)
    starts = ends - own_lengths
    position = jnp.arange(toks, dtype=jnp.int32)[:, None]
    member = ((position >= starts[None, :]) & (position < ends[None, :])).astype(F32)
    own_float = own_lengths.astype(F32)
    seq_of = jnp.sum(member * jnp.arange(seq_dev, dtype=F32)[None, :], axis=1)
    inv_len = jnp.sum(member / own_float[None, :], axis=1)

    slot_iota = jnp.array(slot_order(), jnp.int32)
    at_slot = slot_et[:, None, :] == slot_iota[None, :, None]
    weight_et = (prob * inv_len[:, None]).T
    weight_slot = jnp.sum(jnp.where(at_slot, weight_et[:, None, :], 0.0), axis=2)
    seq_slot = jnp.sum(jnp.where(at_slot, seq_of[None, None, :], 0.0), axis=2)
    side = jnp.concatenate([*split_three(weight_slot), seq_slot.astype(BF16)], axis=1)
    side = jnp.pad(side, ((0, 0), (0, LANES - 4 * cap)))
    side = jnp.pad(side[:, None, :], ((0, 0), (0, MAIN - 1), (0, 0)))
    block_b = jnp.concatenate([gather_rows(mask_b), side], axis=2)
    recv_b = exchange(block_b)

    head_map = jnp.dot(w_down, head_weight, preferred_element_type=F32)
    base = jnp.dot(tokens, head_weight, preferred_element_type=F32)
    base_reward = jnp.sum(base[:, None] * member, axis=0) / own_float

    head_line = head_map[None, :]

    weights = (w_gate, w_up)
    crossed = [swap(w) for w in weights]

    def forward(cap, recv, before, after):
        own = recv.reshape(main_rows, -1)
        other = swap(recv).reshape(main_rows, -1)
        return forward_call(cap, head_number, own, other, *weights, head_line, before, after)

    own_row = jnp.arange(groups, dtype=jnp.int32)[:, None] == me
    base_line = jnp.where(own_row, base_reward[None, :], 0.0).reshape(1, seqs)
    recv_a = touch(recv_a, block_b, head_line, base_line, *crossed)
    dg_a, du_a, score_a = forward(None, recv_a, head_line, head_line)
    grads_a = (dg_a, du_a, swap(dg_a), swap(du_a))
    total_a = backward_call(None, head_number, grads_a, weights, crossed)
    recv_b = touch(recv_b, total_a)
    home_a = exchange(total_a.reshape(groups, MAIN, -1))
    dg_b, du_b, score_b = forward(cap, recv_b, score_a, total_a)
    grads_b = (dg_b, du_b, swap(dg_b), swap(du_b))
    total_b = backward_call(
        cap,
        head_number,
        grads_b,
        weights,
        crossed,
        score_b,
        base_line,
        recv_b.reshape(main_rows, -1),
    )
    total_b = touch(total_b, home_a)
    home_b = exchange(total_b.reshape(groups, MAIN, -1))

    head_half = lax.dynamic_slice_in_dim(head_weight, head * half, half, 0).astype(F32)[None, :]
    acc = pl.pallas_call(
        first_combine_kernel,
        out_shape=jax.ShapeDtypeStruct((toks, half), F32),
        compiler_params=pltpu.CompilerParams(vmem_limit_bytes=24 << 20),
    )(home_a.reshape(main_rows, -1), slot_te, prob, head_half)

    router_half = lax.dynamic_slice_in_dim(router_weight, head * half, half, 0).T
    own_seq = me * seq_dev + jnp.arange(seq_dev, dtype=jnp.int32)
    places = (jnp.arange(seqs, dtype=jnp.int32)[None, :] == own_seq[:, None]).astype(F32)
    member_line = jnp.sum((member / own_float[None, :])[:, :, None] * places[None], axis=1)
    return pl.pallas_call(
        functools.partial(last_combine_kernel, cap),
        out_shape=jax.ShapeDtypeStruct((toks, half), BF16),
        in_specs=[pl.BlockSpec(memory_space=pltpu.VMEM)] + [pl.BlockSpec()] * 9,
        compiler_params=pltpu.CompilerParams(vmem_limit_bytes=24 << 20),
    )(
        home_b.reshape(main_rows, -1),
        slot_te,
        prob,
        slot_ef,
        prob.T,
        acc,
        router_half,
        lengths.astype(F32).reshape(1, seqs),
        pairs,
        member_line,
    )


def solution(mesh):
    return jax.shard_map(
        per_device,
        mesh=mesh,
        in_specs=(
            P("expert", None),
            P(),
            P("expert", None, "head"),
            P("expert", None, "head"),
            P("expert", "head", None),
            P(),
            P("expert", None),
            P(),
            P(),
        ),
        out_specs=P("expert", "head"),
        check_vma=False,
    )
```

```python
import functools

import jax
import jax.numpy as jnp
from jax import lax
from jax.experimental import pallas as pl
from jax.experimental.pallas import tpu as pltpu
from jax.sharding import PartitionSpec as P

LOSS_SCALE = 1024
MAIN = 8
LANES = 128
SWAP = [(0, 1), (1, 0)]
F32 = jnp.float32
BF16 = jnp.bfloat16


def split_three(x):
    high = lax.reduce_precision(x, 8, 7)
    middle = lax.reduce_precision(x - high, 8, 7)
    low = x - high - middle
    return high.astype(BF16), middle.astype(BF16), low.astype(BF16)


def exchange(x):
    return lax.all_to_all(x, "expert", split_axis=0, concat_axis=0, tiled=True)


def swap(x):
    return lax.ppermute(x, "head", SWAP)


def pick(rows, cols, first, axis):
    a = lax.broadcasted_iota(jnp.int32, (rows, cols), axis)
    b = lax.broadcasted_iota(jnp.int32, (rows, cols), 1 - axis)
    return (b == a * MAIN + first).astype(BF16)


def shuffle(rows, groups):
    a = lax.broadcasted_iota(jnp.int32, (rows, rows), 0)
    b = lax.broadcasted_iota(jnp.int32, (rows, rows), 1)
    return (b == (a % groups) * MAIN + a // groups).astype(BF16)


def slot_order():
    return [*range(MAIN), 2 * MAIN, *range(MAIN, 2 * MAIN), 2 * MAIN + 1]


def pieces_of(x):
    high = x.astype(BF16)
    rest = x - high.astype(F32)
    middle = rest.astype(BF16)
    return high, middle, (rest - middle.astype(F32)).astype(BF16)


def spread_pieces(x, cap):
    line = jnp.zeros(x.shape, F32)
    for i, piece in enumerate(pieces_of(x)):
        piece = piece.astype(F32)
        line = line + (pltpu.roll(piece, i * cap, 1) if i else piece)
    return line.astype(BF16)


def join_pieces(line, cap):
    return (
        line + pltpu.roll(line, LANES - cap, 1) + pltpu.roll(line, LANES - 2 * cap, 1)
    )


def touch_kernel(*refs):
    pass


def touch(x, *after, limit=None):
    return pl.pallas_call(
        touch_kernel,
        out_shape=jax.ShapeDtypeStruct(x.shape, x.dtype),
        in_specs=[pl.BlockSpec(memory_space=pl.ANY)] * (1 + len(after)),
        out_specs=pl.BlockSpec(memory_space=pl.ANY),
        input_output_aliases={0: 0},
        compiler_params=pltpu.CompilerParams(vmem_limit_bytes=limit),
    )(x, *after)


def forward_kernel(
    span,
    steps,
    cap,
    head_ref,
    own_hbm,
    other_hbm,
    wg_ref,
    wu_ref,
    hm_ref,
    before_ref,
    after_ref,
    dg_ref,
    du_ref,
    score_ref,
    own_ref,
    other_ref,
    x_ref,
    gate_ref,
    up_ref,
    column_ref,
    stack_ref,
    in_sems,
):
    step = pl.program_id(0)
    main_rows, lanes = own_ref.shape
    groups = main_rows // MAIN
    rows = gate_ref.shape[0]
    halves = steps // 2
    half = halves * span
    piece = half // MAIN
    pieces = span // piece
    own_cols = [slice(i * span, (i + 1) * span) for i in range(halves)] + [slice(half, lanes)]

    def own_in(i):
        cols = own_cols[i]
        return pltpu.make_async_copy(own_hbm.at[:, cols], own_ref.at[:, cols], in_sems.at[i])

    def other_in():
        return pltpu.make_async_copy(other_hbm.at[:, :lanes], other_ref, in_sems.at[halves + 1])

    def gather_extra(src):
        stack_ref[...] = jnp.dot(
            shuffle(main_rows, groups), src[:, half : half + piece], preferred_element_type=F32
        ).astype(BF16)

    def fill(src, chunk):
        x_ref[:main_rows, :] = src[:, chunk * span : (chunk + 1) * span]
        for j in range(pieces):
            q = chunk * pieces + j
            x_ref[main_rows:, j * piece : (j + 1) * piece] = stack_ref[
                q * groups : (q + 1) * groups, :
            ]

    for i in range(steps):

        @pl.when(step == i)
        def _(i=i):
            if i == 0:
                for number in (0, halves, *range(1, halves)):
                    own_in(number).start()
                other_in().start()
                own_in(halves).wait()
                gather_extra(own_ref)
            if i < halves:
                own_in(i).wait()
                fill(own_ref, i)
            else:
                if i == halves:
                    other_in().wait()
                    gather_extra(other_ref)
                fill(other_ref, i - halves)

    @pl.when(step == 0)
    def _():
        gate_ref[...] = jnp.dot(x_ref[...], wg_ref[...], preferred_element_type=F32)
        up_ref[...] = jnp.dot(x_ref[...], wu_ref[...], preferred_element_type=F32)

    @pl.when(step > 0)
    def _():
        gate_ref[...] += jnp.dot(x_ref[...], wg_ref[...], preferred_element_type=F32)
        up_ref[...] += jnp.dot(x_ref[...], wu_ref[...], preferred_element_type=F32)

    @pl.when(step == steps - 1)
    def _():
        block = 64
        head_map = hm_ref[...]

        def body(i, carry):
            here = pl.ds(pl.multiple_of(i * block, block), block)
            gate = gate_ref[here, :]
            up = up_ref[here, :]
            sig = 1.0 / (1.0 + jnp.exp(-gate))
            act = gate * sig
            hidden = (act * up).astype(BF16).astype(F32)
            column_ref[here, :] = jnp.sum(hidden * head_map, axis=1, keepdims=True)
            du_ref[here, :] = (head_map * act).astype(BF16)
            dg_ref[here, :] = (head_map * up * sig * (1.0 + gate * (1.0 - sig))).astype(BF16)
            return carry

        lax.fori_loop(0, rows // block, body, 0)
        place = lax.broadcasted_iota(jnp.int32, (main_rows, LANES), 0) % MAIN
        lane = lax.broadcasted_iota(jnp.int32, (main_rows, LANES), 1)
        table = jnp.where(lane == place, column_ref[:main_rows, :], 0.0)
        a = lax.broadcasted_iota(jnp.int32, (groups, main_rows), 0)
        b = lax.broadcasted_iota(jnp.int32, (groups, main_rows), 1)
        fold = ((b >= a * MAIN) & (b < a * MAIN + MAIN)).astype(BF16)
        folded = sum(jnp.dot(fold, t, preferred_element_type=F32) for t in pieces_of(table))
        lane = lax.broadcasted_iota(jnp.int32, (groups, LANES), 1)
        score = jnp.where(lane == MAIN, column_ref[main_rows:, :], folded)
        if cap is None:
            score_ref[...] = score
        else:
            score = jnp.where(lane <= MAIN, before_ref[...], pltpu.roll(score, MAIN + 1, 1))
            score = jnp.where(lane < cap, score, 0.0)
            score_ref[...] = score
            du_ref[rows:, :] = jnp.zeros((groups, du_ref.shape[1]), BF16)
            du_ref[rows:, :LANES] = spread_pieces(score, cap)


def forward_call(cap, head, own, other, w_gate, w_up, head_map, before, after):
    main_rows = own.shape[0]
    width, hidden = w_gate.shape
    groups = main_rows // MAIN
    half = width // 2
    lanes = half + half // MAIN
    span = 1024
    steps = width // span
    rows = main_rows + groups
    out_rows = rows if cap is None else rows + groups

    def weight_at(i, head_ref):
        return (lax.rem(head_ref[0] * (steps // 2) + i, steps), 0)

    fixed = lambda i, head_ref: (0, 0)
    anywhere = pl.BlockSpec(memory_space=pl.ANY)
    return pl.pallas_call(
        functools.partial(forward_kernel, span, steps, cap),
        grid_spec=pltpu.PrefetchScalarGridSpec(
            num_scalar_prefetch=1,
            grid=(steps,),
            in_specs=[
                anywhere,
                anywhere,
                pl.BlockSpec((span, hidden), weight_at),
                pl.BlockSpec((span, hidden), weight_at),
                pl.BlockSpec((1, hidden), fixed),
                pl.BlockSpec(before.shape, fixed),
                anywhere,
            ],
            out_specs=[
                pl.BlockSpec((rows, hidden), fixed),
                pl.BlockSpec((out_rows, hidden), fixed),
                pl.BlockSpec((groups, LANES), fixed),
            ],
            scratch_shapes=[
                pltpu.VMEM((main_rows, lanes), BF16),
                pltpu.VMEM((main_rows, lanes), BF16),
                pltpu.VMEM((rows, span), BF16),
                pltpu.VMEM((rows, hidden), F32),
                pltpu.VMEM((rows, hidden), F32),
                pltpu.VMEM((rows, 1), F32),
                pltpu.VMEM((main_rows, half // MAIN), BF16),
                pltpu.SemaphoreType.DMA((steps // 2 + 2,)),
            ],
        ),
        out_shape=[
            jax.ShapeDtypeStruct((rows, hidden), BF16),
            jax.ShapeDtypeStruct((out_rows, hidden), BF16),
            jax.ShapeDtypeStruct((groups, LANES), F32),
        ],
        compiler_params=pltpu.CompilerParams(
            dimension_semantics=("arbitrary",), vmem_limit_bytes=62 << 20
        ),
    )(head, own, other, w_gate, w_up, head_map, before, after)


def make_side(cap, own, other, side_in, base, rows):
    groups = own.shape[0]
    seqs = base.shape[1]
    lines = seqs // LANES
    seq_dev = seqs // groups
    lane = lax.broadcasted_iota(jnp.int32, (groups, LANES), 1)
    scores = jnp.where(lane < cap, own + join_pieces(other, cap), 0.0)
    seq_in = pltpu.roll(side_in, LANES - 3 * cap, 1)
    weighted = jnp.where(lane < cap, join_pieces(side_in, cap) * scores, 0.0)
    a = lax.broadcasted_iota(jnp.int32, (groups, seqs), 0)
    b = lax.broadcasted_iota(jnp.int32, (groups, seqs), 1)
    table = jnp.zeros((groups, seqs), F32)
    for j in range(seq_dev):
        part = jnp.sum(jnp.where(seq_in == float(j), weighted, 0.0), axis=1, keepdims=True)
        table = jnp.where(b == a * seq_dev + j, part, table)
    reward = jnp.sum(table, axis=0, keepdims=True) + base
    place = lax.broadcasted_iota(jnp.int32, (rows, LANES), 0) % MAIN
    side = jnp.zeros((rows, LANES), F32)
    for i, piece in enumerate(pieces_of(reward)):
        for line in range(lines):
            values = piece[:, line * LANES : (line + 1) * LANES].astype(F32)
            side = jnp.where(place == i * lines + line, values, side)
    chosen = pick(rows, groups, 3 * lines, 1)
    side = side + jnp.dot(chosen, spread_pieces(scores, cap), preferred_element_type=F32)
    return side.astype(BF16)


def backward_kernel(span, steps, cap, head_ref, *refs):
    if cap is None:
        dg0, du0, dg1, du1, wg0, wu0, wg1, wu1, out_hbm, out_ref, stack_ref, sems = refs
    else:
        (dg0, du0, dg1, du1, wg0, wu0, wg1, wu1, own_ref, base_ref, recv_hbm) = refs[:11]
        out_hbm, out_ref, stack_ref, sems, given_ref = refs[11:]
    step = pl.program_id(0)
    main_rows, lanes = out_ref.shape
    groups = main_rows // MAIN
    rows = dg0.shape[0]
    half = steps * span
    piece = half // MAIN
    pieces = span // piece

    def given():
        return pltpu.make_async_copy(
            recv_hbm.at[:, half + piece :], given_ref, sems.at[steps + 1]
        )

    def leaving(i):
        cols = slice(i * span, (i + 1) * span) if i < steps else slice(half, lanes)
        return pltpu.make_async_copy(out_ref.at[:, cols], out_hbm.at[:, cols], sems.at[i])

    for chunk in range(steps):

        @pl.when(step == chunk)
        def _(chunk=chunk):
            if chunk == 0 and cap is not None:
                given().start()
            dims = (((1,), (1,)), ((), ()))
            value = 0.0
            for grad, weight in ((dg0, wg0), (du0, wu0), (dg1, wg1), (du1, wu1)):
                value = value + lax.dot_general(
                    grad[:rows, :], weight[...], dims, preferred_element_type=F32
                )
            value = value.astype(BF16)
            out_ref[:, chunk * span : (chunk + 1) * span] = value[:main_rows]
            leaving(chunk).start()
            for j in range(pieces):
                q = chunk * pieces + j
                stack_ref[q * groups : (q + 1) * groups, :] = value[
                    main_rows:, j * piece : (j + 1) * piece
                ]
            if chunk == steps - 1:
                out_ref[:, half : half + piece] = lax.dot_general(
                    shuffle(main_rows, groups),
                    stack_ref[...],
                    (((0,), (0,)), ((), ())),
                    preferred_element_type=F32,
                ).astype(BF16)
                if cap is not None:
                    given().wait()
                    side_in = jnp.dot(
                        pick(groups, main_rows, 0, 0), given_ref[...], preferred_element_type=F32
                    )
                    out_ref[:, half + piece :] = make_side(
                        cap,
                        own_ref[...],
                        du1[rows:, :LANES].astype(F32),
                        side_in,
                        base_ref[...],
                        main_rows,
                    )
                leaving(steps).start()
                for number in range(steps + 1):
                    leaving(number).wait()


def backward_call(cap, head, grads, weights, crossed, *side):
    dg = grads[0]
    hidden = dg.shape[1]
    half = weights[0].shape[0] // 2
    span = 512
    steps = half // span
    rows = dg.shape[0]
    main_rows = rows // (MAIN + 1) * MAIN
    lanes = half + half // MAIN + (0 if cap is None else LANES)
    fixed = lambda i, head_ref: (0, 0)
    here = lambda i, head_ref: (head_ref[0] * steps + i, 0)
    anywhere = pl.BlockSpec(memory_space=pl.ANY)
    side_specs = [pl.BlockSpec(x.shape, fixed) for x in side[:-1]] + [anywhere] * len(side[-1:])
    side_scratch = [] if cap is None else [pltpu.VMEM((main_rows, LANES), BF16)]
    return pl.pallas_call(
        functools.partial(backward_kernel, span, steps, cap),
        grid_spec=pltpu.PrefetchScalarGridSpec(
            num_scalar_prefetch=1,
            grid=(steps,),
            in_specs=[pl.BlockSpec(x.shape, fixed) for x in grads]
            + [pl.BlockSpec((span, hidden), here)] * 4
            + side_specs,
            out_specs=anywhere,
            scratch_shapes=[
                pltpu.VMEM((main_rows, lanes), BF16),
                pltpu.VMEM((main_rows, half // MAIN), BF16),
                pltpu.SemaphoreType.DMA((steps + 2,)),
                *side_scratch,
            ],
        ),
        out_shape=jax.ShapeDtypeStruct((main_rows, lanes), BF16),
        compiler_params=pltpu.CompilerParams(
            dimension_semantics=("arbitrary",), vmem_limit_bytes=60 << 20
        ),
    )(head, *grads, *weights, *crossed, *side)


def first_rows_kernel(head_ref, ids_ref, tok_ref, out_ref, slot_ref, buf_ref, stack_ref, sem):
    toks, half = tok_ref.shape
    experts = slot_ref.shape[0]
    rows = out_ref.shape[0]
    piece = half // MAIN
    numbers = lax.broadcasted_iota(jnp.int32, (experts, toks), 0)
    hits = jnp.zeros((experts, toks), F32)
    for k in range(ids_ref.shape[0]):
        hits = jnp.where(ids_ref[k : k + 1, :] == numbers, 1.0, hits)
    a = lax.broadcasted_iota(jnp.int32, (toks, toks), 0)
    b = lax.broadcasted_iota(jnp.int32, (toks, toks), 1)
    before = jnp.dot(hits.astype(BF16), (a < b).astype(BF16), preferred_element_type=F32)
    slot = jnp.where(hits > 0.0, before, -1.0)
    slot_ref[...] = slot
    a = lax.broadcasted_iota(jnp.int32, (rows, experts), 0)
    b = lax.broadcasted_iota(jnp.int32, (rows, experts), 1)
    spread = ((a >= b * MAIN) & (a < b * MAIN + MAIN)).astype(BF16)
    slot_rows = jnp.dot(spread, slot.astype(BF16), preferred_element_type=F32)
    place = lax.broadcasted_iota(jnp.int32, (rows, toks), 0) % MAIN
    main = (slot_rows == place.astype(F32)).astype(BF16)
    in_extra = (slot == float(2 * MAIN)).astype(BF16)
    copies = []
    for q in range(MAIN + 1):
        cols = slice(q * piece, (q + 1) * piece)
        if q < MAIN:
            buf_ref[:, cols] = jnp.dot(
                main, tok_ref[:, cols], preferred_element_type=F32
            ).astype(BF16)
            stack_ref[q * experts : (q + 1) * experts, :] = jnp.dot(
                in_extra, tok_ref[:, cols], preferred_element_type=F32
            ).astype(BF16)
        else:
            dims = (((0,), (0,)), ((), ()))
            buf_ref[:, cols] = lax.dot_general(
                shuffle(rows, experts), stack_ref[...], dims, preferred_element_type=F32
            ).astype(BF16)
        copies.append(pltpu.make_async_copy(buf_ref.at[:, cols], out_ref.at[:, cols], sem.at[q]))
        copies[-1].start()
    for copy in copies:
        copy.wait()


def first_rows(head, ids, tokens, experts):
    toks, width = tokens.shape
    half = width // 2
    rows = experts * MAIN
    lanes = half + half // MAIN
    whole = lambda i, head_ref: (0, 0)
    return pl.pallas_call(
        first_rows_kernel,
        grid_spec=pltpu.PrefetchScalarGridSpec(
            num_scalar_prefetch=1,
            grid=(1,),
            in_specs=[
                pl.BlockSpec(ids.shape, whole),
                pl.BlockSpec((toks, half), lambda i, head_ref: (0, head_ref[0])),
            ],
            out_specs=[
                pl.BlockSpec(memory_space=pl.ANY),
                pl.BlockSpec((experts, toks), whole),
            ],
            scratch_shapes=[
                pltpu.VMEM((rows, lanes), BF16),
                pltpu.VMEM((rows, half // MAIN), BF16),
                pltpu.SemaphoreType.DMA((MAIN + 1,)),
            ],
        ),
        out_shape=[
            jax.ShapeDtypeStruct((rows, lanes), BF16),
            jax.ShapeDtypeStruct((experts, toks), F32),
        ],
        compiler_params=pltpu.CompilerParams(vmem_limit_bytes=60 << 20),
    )(head, ids, tokens)


def combiner(home_ref, slot_te, prob_te, first, extra_slot):
    rows = home_ref.shape[0]
    toks, experts = slot_te.shape
    half = home_ref.shape[1] // (LANES * (MAIN + 1)) * LANES * MAIN
    piece = half // MAIN
    a = lax.broadcasted_iota(jnp.int32, (experts, rows), 0)
    b = lax.broadcasted_iota(jnp.int32, (experts, rows), 1)
    spread = ((b >= a * MAIN) & (b < a * MAIN + MAIN)).astype(BF16)
    column = lax.broadcasted_iota(jnp.int32, (toks, rows), 1) % MAIN

    def repeat(x):
        return jnp.dot(x.astype(BF16), spread, preferred_element_type=F32)

    slot = repeat(slot_te)
    high = prob_te.astype(BF16)
    parts = (repeat(high), repeat(prob_te - high.astype(F32)))
    in_main = slot == (column + first).astype(F32)
    in_extra = slot_te == float(extra_slot)
    main = [jnp.where(in_main, p, 0.0).astype(BF16) for p in parts]

    extra = [
        jnp.where(in_extra, p, 0.0).astype(BF16)
        for p in (high.astype(F32), prob_te - high.astype(F32))
    ]
    stack = jnp.dot(
        shuffle(rows, experts), home_ref[:, half : half + piece], preferred_element_type=F32
    ).astype(BF16)

    def block(index):
        lo = index * 2 * piece
        rows_main = home_ref[:, lo : lo + 2 * piece]
        out = sum(jnp.dot(m, rows_main, preferred_element_type=F32) for m in main)
        sides = []
        for q in (2 * index, 2 * index + 1):
            here = stack[q * experts : (q + 1) * experts]
            sides.append(sum(jnp.dot(m, here, preferred_element_type=F32) for m in extra))
        return out + jnp.concatenate(sides, axis=1)

    return block, 2 * piece


def first_combine_kernel(home_ref, slot_ref, prob_ref, line_ref, out_ref):
    block, width = combiner(home_ref, slot_ref[...], prob_ref[...], 0, 2 * MAIN)
    for i in range(out_ref.shape[1] // width):
        cols = slice(i * width, (i + 1) * width)
        out_ref[:, cols] = block(i) + line_ref[:, cols]


def fit_line(values, seq_lengths):
    n = float(values.shape[1])
    s1 = jnp.sum(seq_lengths, axis=1, keepdims=True)
    s2 = jnp.sum(seq_lengths * seq_lengths, axis=1, keepdims=True)
    v0 = jnp.sum(values, axis=1, keepdims=True)
    v1 = jnp.sum(values * seq_lengths, axis=1, keepdims=True)
    slope = (n * v1 - s1 * v0) / (n * s2 - s1 * s1)
    offset = (v0 - slope * s1) / n
    return values - offset - slope * seq_lengths


def last_combine_kernel(
    cap,
    home_ref,
    slot_ref,
    prob_ref,
    slot_et_ref,
    prob_et_ref,
    acc_ref,
    router_ref,
    lens_ref,
    pairs_ref,
    member_ref,
    out_ref,
):
    rows = home_ref.shape[0]
    experts = rows // MAIN
    seqs = lens_ref.shape[1]
    lines = seqs // LANES
    side = home_ref[:, home_ref.shape[1] - LANES :]
    chosen = pick(experts, rows, 3 * lines, 0)
    packed = jnp.dot(chosen, side, preferred_element_type=F32)
    score_es = join_pieces(packed, cap)
    slot_et = slot_et_ref[...]
    prob_et = prob_et_ref[...]
    score_et = jnp.zeros_like(prob_et)
    for c, number in enumerate(slot_order()):
        score_et = score_et + jnp.where(slot_et == float(number), score_es[:, c : c + 1], 0.0)
    mean_score = jnp.sum(prob_et * score_et, axis=0, keepdims=True)
    dlogits = (prob_et * (score_et - mean_score)).astype(BF16)
    totals = jnp.sum(side.astype(F32).reshape(experts, MAIN, LANES), axis=0)
    totals = totals[:lines] + totals[lines : 2 * lines] + totals[2 * lines : 3 * lines]
    reward = jnp.concatenate([totals[i : i + 1] for i in range(lines)], axis=1)
    lens = lens_ref[...]
    residual = fit_line(reward, lens)
    numbers = lax.broadcasted_iota(jnp.int32, (pairs_ref.shape[0], seqs), 1)
    delta = (numbers == pairs_ref[:, 0:1]).astype(F32) - (numbers == pairs_ref[:, 1:2]).astype(F32)
    margin = jnp.sum(delta * residual, axis=1, keepdims=True)
    pull = LOSS_SCALE / (1.0 + jnp.exp(margin))
    reward_grad = -jnp.sum(pull * delta, axis=0, keepdims=True)
    grad_back = fit_line(reward_grad, lens)
    coef = jnp.sum(member_ref[...] * grad_back, axis=1, keepdims=True)

    block, width = combiner(home_ref, slot_ref[...], prob_ref[...], MAIN, 2 * MAIN + 1)
    for i in range(out_ref.shape[1] // width):
        cols = slice(i * width, (i + 1) * width)
        router_term = lax.dot_general(
            dlogits, router_ref[:, cols], (((0,), (0,)), ((), ())), preferred_element_type=F32
        )
        out_ref[:, cols] = (coef * (block(i) + acc_ref[:, cols] + router_term)).astype(BF16)


def expand(extra_mask, pieces):
    experts, toks = extra_mask.shape
    eye = jnp.eye(pieces, dtype=extra_mask.dtype)
    full = extra_mask[:, None, None, :] * eye[None, :, :, None]
    return full.reshape(experts * pieces, pieces * toks)


def per_device(
    tokens,
    router_weight,
    gate_weight,
    up_weight,
    down_weight,
    head_weight,
    expert_ids,
    lengths,
    pairs,
):
    toks, width = tokens.shape
    experts = router_weight.shape[1]
    groups = lengths.shape[0]
    seq_dev = lengths.shape[1]
    seqs = groups * seq_dev
    half = width // 2
    piece = half // MAIN
    cap = 2 * (MAIN + 1)
    me = lax.axis_index("expert")
    head = lax.axis_index("head")
    w_gate, w_up, w_down = gate_weight[0], up_weight[0], down_weight[0]

    main_rows = groups * MAIN
    head_number = head.astype(jnp.int32)[None]
    block_a, slot_ef = first_rows(head_number, expert_ids.T, tokens, experts)
    slot_te = slot_ef.T
    recv_a = exchange(block_a.reshape(experts, MAIN, -1))
    hits = slot_te >= 0.0
    slot_et = slot_ef.astype(jnp.int32)

    def masks(first, extra):
        slots = first + jnp.arange(MAIN, dtype=jnp.int32)
        main = (slot_et[:, None, :] == slots[None, :, None]).astype(BF16)
        return main.reshape(experts * MAIN, toks), (slot_et == extra).astype(BF16)

    mask_b = masks(MAIN, 2 * MAIN + 1)
    tok_half = lax.dynamic_slice_in_dim(tokens, head * half, half, 1)
    tok_pieces = tok_half.reshape(toks, MAIN, piece).transpose(1, 0, 2).reshape(MAIN * toks, piece)

    def gather_rows(mask):
        main = jnp.dot(mask[0], tok_half, preferred_element_type=F32).astype(BF16)
        extra = jnp.dot(expand(mask[1], MAIN), tok_pieces, preferred_element_type=F32).astype(BF16)
        return jnp.concatenate(
            [main.reshape(experts, MAIN, half), extra.reshape(experts, MAIN, piece)], axis=2
        )


    logits = jnp.dot(tokens, router_weight, preferred_element_type=F32)
    masked = jnp.where(hits, logits, -jnp.inf)
    top = jnp.max(masked, axis=1, keepdims=True)
    weights = jnp.where(hits, jnp.exp(logits - top), 0.0)
    prob = weights / jnp.sum(weights, axis=1, keepdims=True)
    own_lengths = lax.dynamic_slice_in_dim(lengths, me, 1, 0)[0]
    ends = jnp.cumsum(own_lengths)
    starts = ends - own_lengths
    position = jnp.arange(toks, dtype=jnp.int32)[:, None]
    member = ((position >= starts[None, :]) & (position < ends[None, :])).astype(F32)
    own_float = own_lengths.astype(F32)
    seq_of = jnp.sum(member * jnp.arange(seq_dev, dtype=F32)[None, :], axis=1)
    inv_len = jnp.sum(member / own_float[None, :], axis=1)

    slot_iota = jnp.array(slot_order(), jnp.int32)
    at_slot = slot_et[:, None, :] == slot_iota[None, :, None]
    weight_et = (prob * inv_len[:, None]).T
    weight_slot = jnp.sum(jnp.where(at_slot, weight_et[:, None, :], 0.0), axis=2)
    seq_slot = jnp.sum(jnp.where(at_slot, seq_of[None, None, :], 0.0), axis=2)
    side = jnp.concatenate([*split_three(weight_slot), seq_slot.astype(BF16)], axis=1)
    side = jnp.pad(side, ((0, 0), (0, LANES - 4 * cap)))
    side = jnp.pad(side[:, None, :], ((0, 0), (0, MAIN - 1), (0, 0)))
    block_b = jnp.concatenate([gather_rows(mask_b), side], axis=2)

    head_map = jnp.dot(w_down, head_weight, preferred_element_type=F32)
    base = jnp.dot(tokens, head_weight, preferred_element_type=F32)
    base_reward = jnp.sum(base[:, None] * member, axis=0) / own_float

    head_line = head_map[None, :]

    weights = (w_gate, w_up)
    crossed = [swap(w) for w in weights]

    def forward(cap, recv, before, after):
        own = recv.reshape(main_rows, -1)
        other = swap(recv).reshape(main_rows, -1)
        return forward_call(cap, head_number, own, other, *weights, head_line, before, after)

    own_row = jnp.arange(groups, dtype=jnp.int32)[:, None] == me
    base_line = jnp.where(own_row, base_reward[None, :], 0.0).reshape(1, seqs)
    block_b = touch(block_b, head_line, base_line, limit=62 << 20)
    recv_b = exchange(block_b)
    recv_a = touch(recv_a, block_b, *crossed)
    dg_a, du_a, score_a = forward(None, recv_a, head_line, head_line)
    grads_a = (dg_a, du_a, swap(dg_a), swap(du_a))
    total_a = backward_call(None, head_number, grads_a, weights, crossed)
    recv_b = touch(recv_b, total_a)
    home_a = exchange(total_a.reshape(groups, MAIN, -1))
    dg_b, du_b, score_b = forward(cap, recv_b, score_a, total_a)
    grads_b = (dg_b, du_b, swap(dg_b), swap(du_b))
    total_b = backward_call(
        cap,
        head_number,
        grads_b,
        weights,
        crossed,
        score_b,
        base_line,
        recv_b.reshape(main_rows, -1),
    )
    total_b = touch(total_b, home_a)
    home_b = exchange(total_b.reshape(groups, MAIN, -1))

    head_half = lax.dynamic_slice_in_dim(head_weight, head * half, half, 0).astype(F32)[None, :]
    acc = pl.pallas_call(
        first_combine_kernel,
        out_shape=jax.ShapeDtypeStruct((toks, half), F32),
        compiler_params=pltpu.CompilerParams(vmem_limit_bytes=24 << 20),
    )(home_a.reshape(main_rows, -1), slot_te, prob, head_half)

    router_half = lax.dynamic_slice_in_dim(router_weight, head * half, half, 0).T
    own_seq = me * seq_dev + jnp.arange(seq_dev, dtype=jnp.int32)
    places = (jnp.arange(seqs, dtype=jnp.int32)[None, :] == own_seq[:, None]).astype(F32)
    member_line = jnp.sum((member / own_float[None, :])[:, :, None] * places[None], axis=1)
    return pl.pallas_call(
        functools.partial(last_combine_kernel, cap),
        out_shape=jax.ShapeDtypeStruct((toks, half), BF16),
        in_specs=[pl.BlockSpec(memory_space=pltpu.VMEM)] + [pl.BlockSpec()] * 9,
        compiler_params=pltpu.CompilerParams(vmem_limit_bytes=24 << 20),
    )(
        home_b.reshape(main_rows, -1),
        slot_te,
        prob,
        slot_ef,
        prob.T,
        acc,
        router_half,
        lengths.astype(F32).reshape(1, seqs),
        pairs,
        member_line,
    )


def solution(mesh):
    return jax.shard_map(
        per_device,
        mesh=mesh,
        in_specs=(
            P("expert", None),
            P(),
            P("expert", None, "head"),
            P("expert", None, "head"),
            P("expert", "head", None),
            P(),
            P("expert", None),
            P(),
            P(),
        ),
        out_specs=P("expert", "head"),
        check_vma=False,
    )
```

```python
import functools

import jax
import jax.numpy as jnp
from jax import lax
from jax.experimental import pallas as pl
from jax.experimental.pallas import tpu as pltpu
from jax.sharding import PartitionSpec as P

LOSS_SCALE = 1024
MAIN = 8
LANES = 128
SWAP = [(0, 1), (1, 0)]
F32 = jnp.float32
BF16 = jnp.bfloat16


def split_three(x):
    high = lax.reduce_precision(x, 8, 7)
    middle = lax.reduce_precision(x - high, 8, 7)
    low = x - high - middle
    return high.astype(BF16), middle.astype(BF16), low.astype(BF16)


def exchange(x):
    return lax.all_to_all(x, "expert", split_axis=0, concat_axis=0, tiled=True)


def swap(x):
    return lax.ppermute(x, "head", SWAP)


def pick(rows, cols, first, axis):
    a = lax.broadcasted_iota(jnp.int32, (rows, cols), axis)
    b = lax.broadcasted_iota(jnp.int32, (rows, cols), 1 - axis)
    return (b == a * MAIN + first).astype(BF16)


def shuffle(rows, groups):
    a = lax.broadcasted_iota(jnp.int32, (rows, rows), 0)
    b = lax.broadcasted_iota(jnp.int32, (rows, rows), 1)
    return (b == (a % groups) * MAIN + a // groups).astype(BF16)


def slot_order():
    return [*range(MAIN), 2 * MAIN, *range(MAIN, 2 * MAIN), 2 * MAIN + 1]


def pieces_of(x):
    high = x.astype(BF16)
    rest = x - high.astype(F32)
    middle = rest.astype(BF16)
    return high, middle, (rest - middle.astype(F32)).astype(BF16)


def spread_pieces(x, cap):
    line = jnp.zeros(x.shape, F32)
    for i, piece in enumerate(pieces_of(x)):
        piece = piece.astype(F32)
        line = line + (pltpu.roll(piece, i * cap, 1) if i else piece)
    return line.astype(BF16)


def join_pieces(line, cap):
    return (
        line + pltpu.roll(line, LANES - cap, 1) + pltpu.roll(line, LANES - 2 * cap, 1)
    )


def touch_kernel(*refs):
    pass


def touch(x, *after, limit=None):
    return pl.pallas_call(
        touch_kernel,
        out_shape=jax.ShapeDtypeStruct(x.shape, x.dtype),
        in_specs=[pl.BlockSpec(memory_space=pl.ANY)] * (1 + len(after)),
        out_specs=pl.BlockSpec(memory_space=pl.ANY),
        input_output_aliases={0: 0},
        compiler_params=pltpu.CompilerParams(vmem_limit_bytes=limit),
    )(x, *after)


def forward_kernel(
    span,
    steps,
    cap,
    head_ref,
    own_hbm,
    other_hbm,
    wg_ref,
    wu_ref,
    hm_ref,
    before_ref,
    after_ref,
    dg_ref,
    du_ref,
    score_ref,
    own_ref,
    other_ref,
    x_ref,
    gate_ref,
    up_ref,
    column_ref,
    stack_ref,
    in_sems,
):
    step = pl.program_id(0)
    main_rows, lanes = own_ref.shape
    groups = main_rows // MAIN
    rows = gate_ref.shape[0]
    halves = steps // 2
    half = halves * span
    piece = half // MAIN
    pieces = span // piece
    own_cols = [slice(i * span, (i + 1) * span) for i in range(halves)] + [slice(half, lanes)]

    def own_in(i):
        cols = own_cols[i]
        return pltpu.make_async_copy(own_hbm.at[:, cols], own_ref.at[:, cols], in_sems.at[i])

    def other_in():
        return pltpu.make_async_copy(other_hbm.at[:, :lanes], other_ref, in_sems.at[halves + 1])

    def gather_extra(src):
        stack_ref[...] = jnp.dot(
            shuffle(main_rows, groups), src[:, half : half + piece], preferred_element_type=F32
        ).astype(BF16)

    def fill(src, chunk):
        x_ref[:main_rows, :] = src[:, chunk * span : (chunk + 1) * span]
        for j in range(pieces):
            q = chunk * pieces + j
            x_ref[main_rows:, j * piece : (j + 1) * piece] = stack_ref[
                q * groups : (q + 1) * groups, :
            ]

    for i in range(steps):

        @pl.when(step == i)
        def _(i=i):
            if i == 0:
                for number in (0, halves, *range(1, halves)):
                    own_in(number).start()
                other_in().start()
                own_in(halves).wait()
                gather_extra(own_ref)
            if i < halves:
                own_in(i).wait()
                fill(own_ref, i)
            else:
                if i == halves:
                    other_in().wait()
                    gather_extra(other_ref)
                fill(other_ref, i - halves)

    @pl.when(step == 0)
    def _():
        gate_ref[...] = jnp.dot(x_ref[...], wg_ref[...], preferred_element_type=F32)
        up_ref[...] = jnp.dot(x_ref[...], wu_ref[...], preferred_element_type=F32)

    @pl.when(step > 0)
    def _():
        gate_ref[...] += jnp.dot(x_ref[...], wg_ref[...], preferred_element_type=F32)
        up_ref[...] += jnp.dot(x_ref[...], wu_ref[...], preferred_element_type=F32)

    @pl.when(step == steps - 1)
    def _():
        block = 64
        head_map = hm_ref[...]

        def body(i, carry):
            here = pl.ds(pl.multiple_of(i * block, block), block)
            gate = gate_ref[here, :]
            up = up_ref[here, :]
            sig = 1.0 / (1.0 + jnp.exp(-gate))
            act = gate * sig
            hidden = (act * up).astype(BF16).astype(F32)
            column_ref[here, :] = jnp.sum(hidden * head_map, axis=1, keepdims=True)
            du_ref[here, :] = (head_map * act).astype(BF16)
            dg_ref[here, :] = (head_map * up * sig * (1.0 + gate * (1.0 - sig))).astype(BF16)
            return carry

        lax.fori_loop(0, rows // block, body, 0)
        place = lax.broadcasted_iota(jnp.int32, (main_rows, LANES), 0) % MAIN
        lane = lax.broadcasted_iota(jnp.int32, (main_rows, LANES), 1)
        table = jnp.where(lane == place, column_ref[:main_rows, :], 0.0)
        a = lax.broadcasted_iota(jnp.int32, (groups, main_rows), 0)
        b = lax.broadcasted_iota(jnp.int32, (groups, main_rows), 1)
        fold = ((b >= a * MAIN) & (b < a * MAIN + MAIN)).astype(BF16)
        folded = sum(jnp.dot(fold, t, preferred_element_type=F32) for t in pieces_of(table))
        lane = lax.broadcasted_iota(jnp.int32, (groups, LANES), 1)
        score = jnp.where(lane == MAIN, column_ref[main_rows:, :], folded)
        if cap is None:
            score_ref[...] = score
        else:
            score = jnp.where(lane <= MAIN, before_ref[...], pltpu.roll(score, MAIN + 1, 1))
            score = jnp.where(lane < cap, score, 0.0)
            score_ref[...] = score
            du_ref[rows:, :] = jnp.zeros((groups, du_ref.shape[1]), BF16)
            du_ref[rows:, :LANES] = spread_pieces(score, cap)


def forward_call(cap, head, own, other, w_gate, w_up, head_map, before, after):
    main_rows = own.shape[0]
    width, hidden = w_gate.shape
    groups = main_rows // MAIN
    half = width // 2
    lanes = half + half // MAIN
    span = 1024
    steps = width // span
    rows = main_rows + groups
    out_rows = rows if cap is None else rows + groups

    def weight_at(i, head_ref):
        return (lax.rem(head_ref[0] * (steps // 2) + i, steps), 0)

    fixed = lambda i, head_ref: (0, 0)
    anywhere = pl.BlockSpec(memory_space=pl.ANY)
    return pl.pallas_call(
        functools.partial(forward_kernel, span, steps, cap),
        grid_spec=pltpu.PrefetchScalarGridSpec(
            num_scalar_prefetch=1,
            grid=(steps,),
            in_specs=[
                anywhere,
                anywhere,
                pl.BlockSpec((span, hidden), weight_at),
                pl.BlockSpec((span, hidden), weight_at),
                pl.BlockSpec((1, hidden), fixed),
                pl.BlockSpec(before.shape, fixed),
                anywhere,
            ],
            out_specs=[
                pl.BlockSpec((rows, hidden), fixed),
                pl.BlockSpec((out_rows, hidden), fixed),
                pl.BlockSpec((groups, LANES), fixed),
            ],
            scratch_shapes=[
                pltpu.VMEM((main_rows, lanes), BF16),
                pltpu.VMEM((main_rows, lanes), BF16),
                pltpu.VMEM((rows, span), BF16),
                pltpu.VMEM((rows, hidden), F32),
                pltpu.VMEM((rows, hidden), F32),
                pltpu.VMEM((rows, 1), F32),
                pltpu.VMEM((main_rows, half // MAIN), BF16),
                pltpu.SemaphoreType.DMA((steps // 2 + 2,)),
            ],
        ),
        out_shape=[
            jax.ShapeDtypeStruct((rows, hidden), BF16),
            jax.ShapeDtypeStruct((out_rows, hidden), BF16),
            jax.ShapeDtypeStruct((groups, LANES), F32),
        ],
        compiler_params=pltpu.CompilerParams(
            dimension_semantics=("arbitrary",), vmem_limit_bytes=62 << 20
        ),
    )(head, own, other, w_gate, w_up, head_map, before, after)


def make_side(cap, own, other, side_in, base, rows):
    groups = own.shape[0]
    seqs = base.shape[1]
    lines = seqs // LANES
    seq_dev = seqs // groups
    lane = lax.broadcasted_iota(jnp.int32, (groups, LANES), 1)
    scores = jnp.where(lane < cap, own + join_pieces(other, cap), 0.0)
    seq_in = pltpu.roll(side_in, LANES - 3 * cap, 1)
    weighted = jnp.where(lane < cap, join_pieces(side_in, cap) * scores, 0.0)
    a = lax.broadcasted_iota(jnp.int32, (groups, seqs), 0)
    b = lax.broadcasted_iota(jnp.int32, (groups, seqs), 1)
    table = jnp.zeros((groups, seqs), F32)
    for j in range(seq_dev):
        part = jnp.sum(jnp.where(seq_in == float(j), weighted, 0.0), axis=1, keepdims=True)
        table = jnp.where(b == a * seq_dev + j, part, table)
    reward = jnp.sum(table, axis=0, keepdims=True) + base
    place = lax.broadcasted_iota(jnp.int32, (rows, LANES), 0) % MAIN
    side = jnp.zeros((rows, LANES), F32)
    for i, piece in enumerate(pieces_of(reward)):
        for line in range(lines):
            values = piece[:, line * LANES : (line + 1) * LANES].astype(F32)
            side = jnp.where(place == i * lines + line, values, side)
    chosen = pick(rows, groups, 3 * lines, 1)
    side = side + jnp.dot(chosen, spread_pieces(scores, cap), preferred_element_type=F32)
    return side.astype(BF16)


def backward_kernel(span, steps, cap, head_ref, *refs):
    if cap is None:
        dg0, du0, dg1, du1, wg0, wu0, wg1, wu1, out_hbm, out_ref, stack_ref, sems = refs
    else:
        (dg0, du0, dg1, du1, wg0, wu0, wg1, wu1, own_ref, base_ref, recv_hbm) = refs[:11]
        out_hbm, out_ref, stack_ref, sems, given_ref = refs[11:]
    step = pl.program_id(0)
    main_rows, lanes = out_ref.shape
    groups = main_rows // MAIN
    rows = dg0.shape[0]
    half = steps * span
    piece = half // MAIN
    pieces = span // piece

    def given():
        return pltpu.make_async_copy(
            recv_hbm.at[:, half + piece :], given_ref, sems.at[steps + 1]
        )

    def leaving(i):
        cols = slice(i * span, (i + 1) * span) if i < steps else slice(half, lanes)
        return pltpu.make_async_copy(out_ref.at[:, cols], out_hbm.at[:, cols], sems.at[i])

    for chunk in range(steps):

        @pl.when(step == chunk)
        def _(chunk=chunk):
            if chunk == 0 and cap is not None:
                given().start()
            dims = (((1,), (1,)), ((), ()))
            value = 0.0
            for grad, weight in ((dg0, wg0), (du0, wu0), (dg1, wg1), (du1, wu1)):
                value = value + lax.dot_general(
                    grad[:rows, :], weight[...], dims, preferred_element_type=F32
                )
            value = value.astype(BF16)
            out_ref[:, chunk * span : (chunk + 1) * span] = value[:main_rows]
            leaving(chunk).start()
            for j in range(pieces):
                q = chunk * pieces + j
                stack_ref[q * groups : (q + 1) * groups, :] = value[
                    main_rows:, j * piece : (j + 1) * piece
                ]
            if chunk == steps - 1:
                out_ref[:, half : half + piece] = lax.dot_general(
                    shuffle(main_rows, groups),
                    stack_ref[...],
                    (((0,), (0,)), ((), ())),
                    preferred_element_type=F32,
                ).astype(BF16)
                if cap is not None:
                    given().wait()
                    side_in = jnp.dot(
                        pick(groups, main_rows, 0, 0), given_ref[...], preferred_element_type=F32
                    )
                    out_ref[:, half + piece :] = make_side(
                        cap,
                        own_ref[...],
                        du1[rows:, :LANES].astype(F32),
                        side_in,
                        base_ref[...],
                        main_rows,
                    )
                leaving(steps).start()
                for number in range(steps + 1):
                    leaving(number).wait()


def backward_call(cap, head, grads, weights, crossed, *side):
    dg = grads[0]
    hidden = dg.shape[1]
    half = weights[0].shape[0] // 2
    span = 512
    steps = half // span
    rows = dg.shape[0]
    main_rows = rows // (MAIN + 1) * MAIN
    lanes = half + half // MAIN + (0 if cap is None else LANES)
    fixed = lambda i, head_ref: (0, 0)
    here = lambda i, head_ref: (head_ref[0] * steps + i, 0)
    anywhere = pl.BlockSpec(memory_space=pl.ANY)
    side_specs = [pl.BlockSpec(x.shape, fixed) for x in side[:-1]] + [anywhere] * len(side[-1:])
    side_scratch = [] if cap is None else [pltpu.VMEM((main_rows, LANES), BF16)]
    return pl.pallas_call(
        functools.partial(backward_kernel, span, steps, cap),
        grid_spec=pltpu.PrefetchScalarGridSpec(
            num_scalar_prefetch=1,
            grid=(steps,),
            in_specs=[pl.BlockSpec(x.shape, fixed) for x in grads]
            + [pl.BlockSpec((span, hidden), here)] * 4
            + side_specs,
            out_specs=anywhere,
            scratch_shapes=[
                pltpu.VMEM((main_rows, lanes), BF16),
                pltpu.VMEM((main_rows, half // MAIN), BF16),
                pltpu.SemaphoreType.DMA((steps + 2,)),
                *side_scratch,
            ],
        ),
        out_shape=jax.ShapeDtypeStruct((main_rows, lanes), BF16),
        compiler_params=pltpu.CompilerParams(
            dimension_semantics=("arbitrary",), vmem_limit_bytes=60 << 20
        ),
    )(head, *grads, *weights, *crossed, *side)


def first_rows_kernel(head_ref, ids_ref, tok_ref, out_ref, slot_ref, buf_ref, stack_ref, sem):
    toks, half = tok_ref.shape
    experts = slot_ref.shape[0]
    rows = out_ref.shape[0]
    piece = half // MAIN
    numbers = lax.broadcasted_iota(jnp.int32, (experts, toks), 0)
    hits = jnp.zeros((experts, toks), F32)
    for k in range(ids_ref.shape[0]):
        hits = jnp.where(ids_ref[k : k + 1, :] == numbers, 1.0, hits)
    a = lax.broadcasted_iota(jnp.int32, (toks, toks), 0)
    b = lax.broadcasted_iota(jnp.int32, (toks, toks), 1)
    before = jnp.dot(hits.astype(BF16), (a < b).astype(BF16), preferred_element_type=F32)
    slot = jnp.where(hits > 0.0, before, -1.0)
    slot_ref[...] = slot
    a = lax.broadcasted_iota(jnp.int32, (rows, experts), 0)
    b = lax.broadcasted_iota(jnp.int32, (rows, experts), 1)
    spread = ((a >= b * MAIN) & (a < b * MAIN + MAIN)).astype(BF16)
    slot_rows = jnp.dot(spread, slot.astype(BF16), preferred_element_type=F32)
    place = lax.broadcasted_iota(jnp.int32, (rows, toks), 0) % MAIN
    main = (slot_rows == place.astype(F32)).astype(BF16)
    in_extra = (slot == float(2 * MAIN)).astype(BF16)
    copies = []
    for q in range(MAIN + 1):
        cols = slice(q * piece, (q + 1) * piece)
        if q < MAIN:
            buf_ref[:, cols] = jnp.dot(
                main, tok_ref[:, cols], preferred_element_type=F32
            ).astype(BF16)
            stack_ref[q * experts : (q + 1) * experts, :] = jnp.dot(
                in_extra, tok_ref[:, cols], preferred_element_type=F32
            ).astype(BF16)
        else:
            dims = (((0,), (0,)), ((), ()))
            buf_ref[:, cols] = lax.dot_general(
                shuffle(rows, experts), stack_ref[...], dims, preferred_element_type=F32
            ).astype(BF16)
        copies.append(pltpu.make_async_copy(buf_ref.at[:, cols], out_ref.at[:, cols], sem.at[q]))
        copies[-1].start()
    for copy in copies:
        copy.wait()


def first_rows(head, ids, tokens, experts):
    toks, width = tokens.shape
    half = width // 2
    rows = experts * MAIN
    lanes = half + half // MAIN
    whole = lambda i, head_ref: (0, 0)
    return pl.pallas_call(
        first_rows_kernel,
        grid_spec=pltpu.PrefetchScalarGridSpec(
            num_scalar_prefetch=1,
            grid=(1,),
            in_specs=[
                pl.BlockSpec(ids.shape, whole),
                pl.BlockSpec((toks, half), lambda i, head_ref: (0, head_ref[0])),
            ],
            out_specs=[
                pl.BlockSpec(memory_space=pl.ANY),
                pl.BlockSpec((experts, toks), whole),
            ],
            scratch_shapes=[
                pltpu.VMEM((rows, lanes), BF16),
                pltpu.VMEM((rows, half // MAIN), BF16),
                pltpu.SemaphoreType.DMA((MAIN + 1,)),
            ],
        ),
        out_shape=[
            jax.ShapeDtypeStruct((rows, lanes), BF16),
            jax.ShapeDtypeStruct((experts, toks), F32),
        ],
        compiler_params=pltpu.CompilerParams(vmem_limit_bytes=60 << 20),
    )(head, ids, tokens)


def combiner(home_ref, slot_te, prob_te, first, extra_slot):
    rows = home_ref.shape[0]
    toks, experts = slot_te.shape
    half = home_ref.shape[1] // (LANES * (MAIN + 1)) * LANES * MAIN
    piece = half // MAIN
    a = lax.broadcasted_iota(jnp.int32, (experts, rows), 0)
    b = lax.broadcasted_iota(jnp.int32, (experts, rows), 1)
    spread = ((b >= a * MAIN) & (b < a * MAIN + MAIN)).astype(BF16)
    column = lax.broadcasted_iota(jnp.int32, (toks, rows), 1) % MAIN

    def repeat(x):
        return jnp.dot(x.astype(BF16), spread, preferred_element_type=F32)

    slot = repeat(slot_te)
    high = prob_te.astype(BF16)
    parts = (repeat(high), repeat(prob_te - high.astype(F32)))
    in_main = slot == (column + first).astype(F32)
    in_extra = slot_te == float(extra_slot)
    main = [jnp.where(in_main, p, 0.0).astype(BF16) for p in parts]

    extra = [
        jnp.where(in_extra, p, 0.0).astype(BF16)
        for p in (high.astype(F32), prob_te - high.astype(F32))
    ]
    stack = jnp.dot(
        shuffle(rows, experts), home_ref[:, half : half + piece], preferred_element_type=F32
    ).astype(BF16)

    def block(index):
        lo = index * 2 * piece
        rows_main = home_ref[:, lo : lo + 2 * piece]
        out = sum(jnp.dot(m, rows_main, preferred_element_type=F32) for m in main)
        sides = []
        for q in (2 * index, 2 * index + 1):
            here = stack[q * experts : (q + 1) * experts]
            sides.append(sum(jnp.dot(m, here, preferred_element_type=F32) for m in extra))
        return out + jnp.concatenate(sides, axis=1)

    return block, 2 * piece


def first_combine_kernel(home_ref, slot_ref, prob_ref, line_ref, out_ref):
    block, width = combiner(home_ref, slot_ref[...], prob_ref[...], 0, 2 * MAIN)
    for i in range(out_ref.shape[1] // width):
        cols = slice(i * width, (i + 1) * width)
        out_ref[:, cols] = block(i) + line_ref[:, cols]


def fit_line(values, seq_lengths):
    n = float(values.shape[1])
    s1 = jnp.sum(seq_lengths, axis=1, keepdims=True)
    s2 = jnp.sum(seq_lengths * seq_lengths, axis=1, keepdims=True)
    v0 = jnp.sum(values, axis=1, keepdims=True)
    v1 = jnp.sum(values * seq_lengths, axis=1, keepdims=True)
    slope = (n * v1 - s1 * v0) / (n * s2 - s1 * s1)
    offset = (v0 - slope * s1) / n
    return values - offset - slope * seq_lengths


def last_combine_kernel(
    cap,
    home_ref,
    slot_ref,
    prob_ref,
    slot_et_ref,
    prob_et_ref,
    acc_ref,
    router_ref,
    lens_ref,
    pairs_ref,
    member_ref,
    out_ref,
):
    rows = home_ref.shape[0]
    experts = rows // MAIN
    seqs = lens_ref.shape[1]
    lines = seqs // LANES
    side = home_ref[:, home_ref.shape[1] - LANES :]
    chosen = pick(experts, rows, 3 * lines, 0)
    packed = jnp.dot(chosen, side, preferred_element_type=F32)
    score_es = join_pieces(packed, cap)
    slot_et = slot_et_ref[...]
    prob_et = prob_et_ref[...]
    score_et = jnp.zeros_like(prob_et)
    for c, number in enumerate(slot_order()):
        score_et = score_et + jnp.where(slot_et == float(number), score_es[:, c : c + 1], 0.0)
    mean_score = jnp.sum(prob_et * score_et, axis=0, keepdims=True)
    dlogits = (prob_et * (score_et - mean_score)).astype(BF16)
    totals = jnp.sum(side.astype(F32).reshape(experts, MAIN, LANES), axis=0)
    totals = totals[:lines] + totals[lines : 2 * lines] + totals[2 * lines : 3 * lines]
    reward = jnp.concatenate([totals[i : i + 1] for i in range(lines)], axis=1)
    lens = lens_ref[...]
    residual = fit_line(reward, lens)
    numbers = lax.broadcasted_iota(jnp.int32, (pairs_ref.shape[0], seqs), 1)
    delta = (numbers == pairs_ref[:, 0:1]).astype(F32) - (numbers == pairs_ref[:, 1:2]).astype(F32)
    margin = jnp.sum(delta * residual, axis=1, keepdims=True)
    pull = LOSS_SCALE / (1.0 + jnp.exp(margin))
    reward_grad = -jnp.sum(pull * delta, axis=0, keepdims=True)
    grad_back = fit_line(reward_grad, lens)
    coef = jnp.sum(member_ref[...] * grad_back, axis=1, keepdims=True)

    block, width = combiner(home_ref, slot_ref[...], prob_ref[...], MAIN, 2 * MAIN + 1)
    for i in range(out_ref.shape[1] // width):
        cols = slice(i * width, (i + 1) * width)
        router_term = lax.dot_general(
            dlogits, router_ref[:, cols], (((0,), (0,)), ((), ())), preferred_element_type=F32
        )
        out_ref[:, cols] = (coef * (block(i) + acc_ref[:, cols] + router_term)).astype(BF16)


def expand(extra_mask, pieces):
    experts, toks = extra_mask.shape
    eye = jnp.eye(pieces, dtype=extra_mask.dtype)
    full = extra_mask[:, None, None, :] * eye[None, :, :, None]
    return full.reshape(experts * pieces, pieces * toks)


def per_device(
    tokens,
    router_weight,
    gate_weight,
    up_weight,
    down_weight,
    head_weight,
    expert_ids,
    lengths,
    pairs,
):
    toks, width = tokens.shape
    experts = router_weight.shape[1]
    groups = lengths.shape[0]
    seq_dev = lengths.shape[1]
    seqs = groups * seq_dev
    half = width // 2
    piece = half // MAIN
    cap = 2 * (MAIN + 1)
    me = lax.axis_index("expert")
    head = lax.axis_index("head")
    w_gate, w_up, w_down = gate_weight[0], up_weight[0], down_weight[0]

    main_rows = groups * MAIN
    head_number = head.astype(jnp.int32)[None]
    block_a, slot_ef = first_rows(head_number, expert_ids.T, tokens, experts)
    slot_te = slot_ef.T
    recv_a = exchange(block_a.reshape(experts, MAIN, -1))
    hits = slot_te >= 0.0
    slot_et = slot_ef.astype(jnp.int32)

    def masks(first, extra):
        slots = first + jnp.arange(MAIN, dtype=jnp.int32)
        main = (slot_et[:, None, :] == slots[None, :, None]).astype(BF16)
        return main.reshape(experts * MAIN, toks), (slot_et == extra).astype(BF16)

    mask_b = masks(MAIN, 2 * MAIN + 1)
    tok_half = lax.dynamic_slice_in_dim(tokens, head * half, half, 1)
    tok_pieces = tok_half.reshape(toks, MAIN, piece).transpose(1, 0, 2).reshape(MAIN * toks, piece)

    def gather_rows(mask):
        main = jnp.dot(mask[0], tok_half, preferred_element_type=F32).astype(BF16)
        extra = jnp.dot(expand(mask[1], MAIN), tok_pieces, preferred_element_type=F32).astype(BF16)
        return jnp.concatenate(
            [main.reshape(experts, MAIN, half), extra.reshape(experts, MAIN, piece)], axis=2
        )


    logits = jnp.dot(tokens, router_weight, preferred_element_type=F32)
    masked = jnp.where(hits, logits, -jnp.inf)
    top = jnp.max(masked, axis=1, keepdims=True)
    weights = jnp.where(hits, jnp.exp(logits - top), 0.0)
    prob = weights / jnp.sum(weights, axis=1, keepdims=True)
    own_lengths = lax.dynamic_slice_in_dim(lengths, me, 1, 0)[0]
    ends = jnp.cumsum(own_lengths)
    starts = ends - own_lengths
    position = jnp.arange(toks, dtype=jnp.int32)[:, None]
    member = ((position >= starts[None, :]) & (position < ends[None, :])).astype(F32)
    own_float = own_lengths.astype(F32)
    seq_of = jnp.sum(member * jnp.arange(seq_dev, dtype=F32)[None, :], axis=1)
    inv_len = jnp.sum(member / own_float[None, :], axis=1)

    slot_iota = jnp.array(slot_order(), jnp.int32)
    at_slot = slot_et[:, None, :] == slot_iota[None, :, None]
    weight_et = (prob * inv_len[:, None]).T
    weight_slot = jnp.sum(jnp.where(at_slot, weight_et[:, None, :], 0.0), axis=2)
    seq_slot = jnp.sum(jnp.where(at_slot, seq_of[None, None, :], 0.0), axis=2)
    side = jnp.concatenate([*split_three(weight_slot), seq_slot.astype(BF16)], axis=1)
    side = jnp.pad(side, ((0, 0), (0, LANES - 4 * cap)))
    side = jnp.pad(side[:, None, :], ((0, 0), (0, MAIN - 1), (0, 0)))
    block_b = jnp.concatenate([gather_rows(mask_b), side], axis=2)

    head_map = jnp.dot(w_down, head_weight, preferred_element_type=F32)
    base = jnp.dot(tokens, head_weight, preferred_element_type=F32)
    base_reward = jnp.sum(base[:, None] * member, axis=0) / own_float

    head_line = head_map[None, :]

    weights = (w_gate, w_up)
    crossed = [swap(w) for w in weights]

    def forward(cap, recv, before, after):
        own = recv.reshape(main_rows, -1)
        other = swap(recv).reshape(main_rows, -1)
        return forward_call(cap, head_number, own, other, *weights, head_line, before, after)

    own_row = jnp.arange(groups, dtype=jnp.int32)[:, None] == me
    base_line = jnp.where(own_row, base_reward[None, :], 0.0).reshape(1, seqs)
    block_b = touch(block_b, head_line, base_line, limit=62 << 20)
    recv_b = exchange(block_b)
    recv_a = touch(recv_a, block_b, *crossed)
    dg_a, du_a, score_a = forward(None, recv_a, head_line, head_line)
    grads_a = (dg_a, du_a, swap(dg_a), swap(du_a))
    total_a = backward_call(None, head_number, grads_a, weights, crossed)
    recv_b = touch(recv_b, total_a)
    home_a = exchange(total_a.reshape(groups, MAIN, -1))
    dg_b, du_b, score_b = forward(cap, recv_b, score_a, total_a)
    score_b = touch(score_b, limit=127 << 19)
    grads_b = (dg_b, du_b, swap(dg_b), swap(du_b))
    total_b = backward_call(
        cap,
        head_number,
        grads_b,
        weights,
        crossed,
        score_b,
        base_line,
        recv_b.reshape(main_rows, -1),
    )
    total_b = touch(total_b, home_a)
    home_b = exchange(total_b.reshape(groups, MAIN, -1))

    head_half = lax.dynamic_slice_in_dim(head_weight, head * half, half, 0).astype(F32)[None, :]
    acc = pl.pallas_call(
        first_combine_kernel,
        out_shape=jax.ShapeDtypeStruct((toks, half), F32),
        compiler_params=pltpu.CompilerParams(vmem_limit_bytes=24 << 20),
    )(home_a.reshape(main_rows, -1), slot_te, prob, head_half)

    router_half = lax.dynamic_slice_in_dim(router_weight, head * half, half, 0).T
    own_seq = me * seq_dev + jnp.arange(seq_dev, dtype=jnp.int32)
    places = (jnp.arange(seqs, dtype=jnp.int32)[None, :] == own_seq[:, None]).astype(F32)
    member_line = jnp.sum((member / own_float[None, :])[:, :, None] * places[None], axis=1)
    return pl.pallas_call(
        functools.partial(last_combine_kernel, cap),
        out_shape=jax.ShapeDtypeStruct((toks, half), BF16),
        in_specs=[pl.BlockSpec(memory_space=pltpu.VMEM)] + [pl.BlockSpec()] * 9,
        compiler_params=pltpu.CompilerParams(vmem_limit_bytes=24 << 20),
    )(
        home_b.reshape(main_rows, -1),
        slot_te,
        prob,
        slot_ef,
        prob.T,
        acc,
        router_half,
        lengths.astype(F32).reshape(1, seqs),
        pairs,
        member_line,
    )


def solution(mesh):
    return jax.shard_map(
        per_device,
        mesh=mesh,
        in_specs=(
            P("expert", None),
            P(),
            P("expert", None, "head"),
            P("expert", None, "head"),
            P("expert", "head", None),
            P(),
            P("expert", None),
            P(),
            P(),
        ),
        out_specs=P("expert", "head"),
        check_vma=False,
    )
```
